128 devices in a mesh: dp: 32 (over y, x, core), task: 4 (over z).
Axes of the slice: x: 4, y: 4, z: 4, core: 2. Of those that a mesh axis runs over, the one named last changes fastest.
Arguments:
- residual: bfloat16 [128, 128, 1920], P(('dp', 'task')), may hold values from -6 to 6
- attn_output: bfloat16 [128, 128, 1920], P(('dp', 'task')), may hold values from -6 to 6
- out_weight: bfloat16 [1920, 1920], P(('dp', 'task')), may hold values from -0.125 to 0.125
- norm_gain: float32 [1920], replicated, may hold values from 0.1 to 1.9
- head_deconv: bfloat16 [3, 1920, 1280], P(None, 'dp', 'task'), may hold values from -0.125 to 0.125
- classifier: bfloat16 [320, 32], replicated, may hold values from -0.59765625 to 0.59765625
- labels: int32 [128, 3], replicated, may hold values from 0 to 1, as said below
- counts: int32 [3], replicated, may hold values from 16 to 96, as said below
- cotangent: bfloat16 [128, 128, 128], P(('dp', 'task')), may hold values from -6 to 6
Outputs:
- grad_residual: float32 [128, 128, 1920], P(('dp', 'task'))
- grad_attention: bfloat16 [128, 128, 1920], P(('dp', 'task'))
- grad_out_weight: float32 [1920, 1920], P(('dp', 'task'))
- grad_deconv: float32 [3, 1920, 1280], P(None, 'dp', 'task')
- grad_classifier: float32 [320, 32], replicated
The draws below stay inside these ranges and needn't reach their ends.
Inputs may be any that keep to these rules, and one draw needn't show every extreme that they name: `labels`: one task is carried by exactly 96 samples, another by exactly 48, the third by 16 to 48; which task is which is drawn. counts[t] is the number of samples s with labels[s, t] = 1.
All inputs are finite; a program needn't handle non-finite values.
Results may differ from the reference program's by a relative error of at most 0.008.
Values may be sent and summed in bfloat16 or wider, within the bound.
No kernel may reach another device: no remote copies, remote signals or barrier semaphores. Data moves between devices by JAX's collectives and lax.ppermute only.
A program may use at most 128 MiB of HBM per device.

```python
import jax
import jax.numpy as jnp
from jax import lax

D = 1920
HC = 320
KT = 32
TOKW = 128
SAMPLES = 128
MOSTS = 96


def label_table(key):
    ordering = jax.random.permutation(jax.random.fold_in(key, 11), 3)
    third_size = jax.random.randint(jax.random.fold_in(key, 12), (), SAMPLES // 8, MOSTS // 2 + 1)
    task_sizes = jnp.zeros((3,), jnp.int32).at[ordering].set(jnp.stack([jnp.int32(MOSTS), jnp.int32(MOSTS // 2), third_size.astype(jnp.int32)]))
    label_columns = []
    for task_index in range(3):
        shuffled = jax.random.permutation(jax.random.fold_in(key, 20 + task_index), SAMPLES)
        position = jnp.zeros((SAMPLES,), jnp.int32).at[shuffled].set(jnp.arange(SAMPLES, dtype=jnp.int32))
        label_columns.append((position < task_sizes[task_index]).astype(jnp.int32))
    return (jnp.stack(label_columns, 1), task_sizes)


def draw_labels(key, part):
    label_grid, task_sizes = label_table(key)
    return label_grid


def draw_counts(key, part):
    label_grid, task_sizes = label_table(key)
    return task_sizes


def block_levels(rng, dims, pieces, low, largest):
    def one(dim, parts):
        steps = jax.random.uniform(jax.random.fold_in(jax.random.fold_in(rng, 6), dim), (parts,), jnp.float32, low / len(pieces), largest / len(pieces))
        return jnp.repeat(jnp.exp(steps), dims[dim] // parts).reshape((-1,) + (1,) * (len(dims) - dim - 1))

    factor_of = one(*pieces[0])
    for cut in pieces[1:]:
        factor_of = factor_of * one(*cut)
    return factor_of


def noise(stream_key, shape, spread, limit, split=(), held_as=jnp.bfloat16):
    entries = jax.random.normal(stream_key, shape, jnp.float32) * spread
    if len(split) > 0:
        entries = block_levels(stream_key, shape, split, -0.22, 0.18) * entries
    return jnp.clip(entries, min=-limit, max=limit).astype(held_as)


def setup_inputs(seed: int = 0) -> dict:
    keys = jax.random.split(jax.random.key(seed), 10)
    residual = noise(keys[0], (SAMPLES, TOKW, D), 1.0, 6.0, ((0, 128),))
    attn_output = noise(keys[1], (SAMPLES, TOKW, D), 1.0, 6.0, ((0, 128),))
    out_weight = noise(keys[2], (D, D), D ** -0.5, 0.125, ((0, 128),))
    norm_gain = jnp.clip(1.0 + 0.18 * jax.random.normal(keys[3], (D,), jnp.float32), 0.1, 1.9)
    head_deconv = noise(keys[4], (3, D, 4 * HC), D ** -0.5, 0.125, ((1, 32), (2, 4)))
    classifier = noise(keys[5], (HC, KT), 0.1, 0.59765625)
    labels = draw_labels(jax.random.fold_in(keys[9], 71), 0)
    counts = draw_counts(jax.random.fold_in(keys[9], 71), 0)
    cotangent = noise(keys[8], (SAMPLES, TOKW, 4 * KT), 1.0, 6.0, ((0, 128),))
    return {"residual": residual, "attn_output": attn_output, "out_weight": out_weight, "norm_gain": norm_gain, "head_deconv": head_deconv, "classifier": classifier, "labels": labels, "counts": counts, "cotangent": cotangent}


def silu_slope(values):
    sigmoid_value = jax.nn.sigmoid(values)
    return sigmoid_value * (1.0 + values * (1.0 - sigmoid_value))

def reference(residual, attn_output, out_weight, norm_gain, head_deconv, classifier, labels, counts, cotangent):
    rows_all = SAMPLES * TOKW
    attention = attn_output.reshape(rows_all, D)
    stream = residual.reshape(rows_all, D).astype(jnp.float32) + jnp.dot(attention, out_weight, preferred_element_type=jnp.float32)
    center = stream - lax.optimization_barrier(jnp.mean(stream, axis=1, keepdims=True))
    inverse = lax.rsqrt(lax.optimization_barrier(jnp.mean(center * center, axis=1, keepdims=True)) + 1e-06)
    normed = center * inverse
    features = (normed * norm_gain).astype(jnp.bfloat16)
    flat_cot = cotangent.reshape(rows_all, 4 * KT).astype(jnp.float32)
    column = jnp.arange(4 * KT) % KT
    lower_cols = [0, 1, 4]
    upper_cols = [1, 4, KT]
    task_weight = SAMPLES / (3.0 * counts.astype(jnp.float32))
    feature_grad = jnp.zeros((rows_all, D), jnp.float32)
    class_grad = jnp.zeros((HC, KT), jnp.float32)
    deconv_list = []
    for task_index in range(3):
        row_scale = jnp.repeat(labels[:, task_index].astype(jnp.float32) * task_weight[task_index], TOKW)
        col_mask = ((column >= lower_cols[task_index]) & (column < upper_cols[task_index])).astype(jnp.float32)
        grad_pred = (flat_cot * row_scale[:, None] * col_mask[None, :]).astype(jnp.bfloat16)
        pre_act = jnp.dot(features, head_deconv[task_index], preferred_element_type=jnp.float32)
        activation = jax.nn.silu(pre_act).astype(jnp.bfloat16)
        grad_act = jnp.einsum('rqk,ck->rqc', grad_pred.reshape(rows_all, 4, KT).astype(jnp.float32), classifier.astype(jnp.float32)).reshape(rows_all, 4 * HC)
        grad_pre = (grad_act * silu_slope(pre_act)).astype(jnp.bfloat16)
        class_grad = class_grad + jnp.einsum('rqc,rqk->ck', activation.reshape(rows_all, 4, HC).astype(jnp.float32), grad_pred.reshape(rows_all, 4, KT).astype(jnp.float32))
        deconv_list.append(jnp.dot(features.T, grad_pre, preferred_element_type=jnp.float32))
        feature_term = jnp.dot(grad_pre, head_deconv[task_index].T, preferred_element_type=jnp.float32).astype(jnp.bfloat16)
        feature_term = lax.optimization_barrier(feature_term)
        feature_grad = feature_grad + feature_term.astype(jnp.float32)
    scaled = feature_grad * norm_gain
    stream_grad = inverse * (scaled - lax.optimization_barrier(jnp.mean(scaled, axis=1, keepdims=True)) - normed * lax.optimization_barrier(jnp.mean(scaled * normed, axis=1, keepdims=True)))
    stream_bf = stream_grad.astype(jnp.bfloat16)
    grad_attention = jnp.dot(stream_bf, out_weight.T, preferred_element_type=jnp.float32).astype(jnp.bfloat16)
    weight_grad = jnp.dot(attention.T, stream_bf, preferred_element_type=jnp.float32)
    return (stream_grad.reshape(SAMPLES, TOKW, D), grad_attention.reshape(SAMPLES, TOKW, D), weight_grad, jnp.stack(deconv_list), class_grad)
```

```python
import jax
import jax.numpy as jnp
from jax import lax
from jax.sharding import Mesh, PartitionSpec as P

BF = jnp.bfloat16
F32 = jnp.float32
OFFSETS = (0, 3, 1, 2)
ORDER = ("z", "y", "x")
ROUTES = (("x", "y", "z"), ("y", "z", "x"), ("z", "x", "y"))
CUTS = ((0, 768), (768, 1408), (1408, 2048))
LANE_ROWS = 16


def shift(value, axis, by):
    size = lax.axis_size(axis)
    return lax.ppermute(value, axis, [(i, (i + by) % size) for i in range(size)])


def gather_axis(piece, axis, dim):
    parts = [piece] + [shift(piece, axis, -off) for off in OFFSETS[1:]]
    return jnp.concatenate(parts, axis=dim)


def scatter_axis(value, axis, dim):
    mine = lax.index_in_dim(value, 0, dim, keepdims=True).astype(F32)
    for digit, off in enumerate(OFFSETS[1:], 1):
        block = lax.index_in_dim(value, digit, dim, keepdims=True).astype(BF)
        mine = mine + shift(block, axis, off).astype(F32)
    return mine


def dot(a, b, ca, cb):
    return lax.dot_general(a, b, (((ca,), (cb,)), ((), ())), preferred_element_type=F32)


def silu_slope(values):
    sigmoid_value = jax.nn.sigmoid(values)
    return sigmoid_value * (1.0 + values * (1.0 - sigmoid_value))


def per_device(
    residual, attn_output, out_weight, norm_gain, head_deconv, classifier, labels, counts, cotangent
):
    at = {name: lax.axis_index(name) for name in ("y", "x", "c", "z")}
    samples = labels.shape[0]
    attention = attn_output[0]
    tokens, width = attention.shape
    hidden, classes = classifier.shape
    rows_dp = head_deconv.shape[1]
    pad_dp = 64
    groups = width // rows_dp
    wide = groups * pad_dp
    own_rows = out_weight.shape[0]

    padded = jnp.arange(wide)
    source = jnp.where(padded % pad_dp < rows_dp, padded // pad_dp * rows_dp + padded % pad_dp, -1)
    spread = (jnp.arange(width)[:, None] == source[None, :]).astype(BF)
    mask = (source >= 0).astype(F32)
    gain = jnp.pad(norm_gain.reshape(groups, rows_dp), ((0, 0), (0, pad_dp - rows_dp))).reshape(wide)

    piece = jnp.pad(dot(out_weight, spread, 1, 0).astype(BF), ((0, LANE_ROWS - own_rows), (0, 0)))
    weight_parts = []
    for route, (lo, hi) in zip(ROUTES, CUTS):
        block = piece[:, lo:hi].reshape(1, 1, 1, LANE_ROWS, hi - lo)
        for axis in route:
            block = gather_axis(block, axis, ORDER.index(axis))
        weight_parts.append(block.reshape(64 * LANE_ROWS, hi - lo))
    weight = jnp.concatenate(weight_parts, axis=1)

    heads_local = jnp.pad(
        jnp.transpose(head_deconv, (1, 0, 2)).reshape(rows_dp, -1), ((0, pad_dp - rows_dp), (0, 0))
    )
    heads = lax.all_gather(heads_local, ("y", "x", "c"), axis=0, tiled=True)

    row = jnp.arange(64 * LANE_ROWS)
    table = jnp.array(OFFSETS, jnp.int32)
    digit = {
        name: (at[name] + table[(row // (LANE_ROWS * 4 ** (2 - i))) % 4]) % 4
        for i, name in enumerate(ORDER)
    }
    sub = row % LANE_ROWS

    def select_for(core):
        target = ((digit["y"] * 4 + digit["x"]) * 2 + core) * 4 * own_rows + digit["z"] * own_rows + sub
        target = jnp.where(sub < own_rows, target, -1)
        return (jnp.arange(width)[:, None] == target[None, :]).astype(BF)

    pick_here = select_for(at["c"])
    pick_there = select_for(1 - at["c"])
    attn_pair = jnp.concatenate([attention, shift(attention, "c", 1)], axis=0)
    attn_cols = dot(attn_pair, pick_here, 1, 0).astype(BF)
    residual_wide = dot(residual[0], spread, 1, 0)

    cot_blocks = []
    label_rows = []
    for off in OFFSETS:
        cut = lax.dynamic_slice_in_dim(cotangent[0], ((at["z"] - off) % 4) * classes, classes, 1)
        cot_blocks.append(cut if off == 0 else shift(cut, "z", -off))
        index = ((at["y"] * 4 + at["x"]) * 2 + at["c"]) * 4 + (at["z"] + off) % 4
        label_rows.append(lax.dynamic_slice_in_dim(labels, index, 1, 0))
    task_weight = samples / (3.0 * counts.astype(F32))
    column = jnp.arange(classes)
    column_task = (column >= 1).astype(jnp.int32) + (column >= 4).astype(jnp.int32)
    column_hot = (column_task[None, :] == jnp.arange(3)[:, None]).astype(F32)
    column_weight = jnp.sum(column_hot * task_weight[:, None], axis=0)
    label_mask = jnp.sum(
        jnp.concatenate(label_rows, 0).astype(F32)[:, :, None] * column_hot[None], axis=1
    )
    pred_grad = (
        jnp.stack(cot_blocks).astype(F32) * (label_mask * column_weight[None, :])[:, None, :]
    ).astype(BF).reshape(4 * tokens, classes)
    class_wide = (
        jnp.transpose(classifier).astype(F32)[:, None, :] * jnp.transpose(column_hot)[:, :, None]
    ).astype(BF).reshape(classes, 3 * hidden)
    act_grad = dot(pred_grad, class_wide, 1, 0)

    product = dot(attn_cols, weight, 1, 0)
    stream = residual_wide + product[:tokens] + shift(product[tokens:].astype(BF), "c", 1).astype(F32)
    center = (stream - jnp.sum(stream, axis=1, keepdims=True) / width) * mask
    inverse = lax.rsqrt(jnp.sum(center * center, axis=1, keepdims=True) / width + 1e-06)
    normed = center * inverse
    features = (normed * gain).astype(BF)
    feats = gather_axis(features, "z", 0)

    pre_act = dot(feats, heads, 1, 0)
    activation = jax.nn.silu(pre_act).astype(BF)
    pre_grad = (act_grad * silu_slope(pre_act)).astype(BF)
    back = dot(pre_grad, heads, 1, 1)
    feature_grad = scatter_axis(back.reshape(4, tokens, wide), "z", 0)[0]

    class_part = dot(activation, pred_grad, 0, 0).reshape(3, hidden, classes)
    class_total = lax.psum(jnp.sum(class_part * column_hot[:, None, :], axis=0), ("y", "x", "c", "z"))

    deconv_part = dot(feats, pre_grad, 0, 0).astype(BF).reshape(16, 2, pad_dp, 3 * hidden)
    send = lax.dynamic_slice_in_dim(deconv_part, 1 - at["c"], 1, 1)[:, 0]
    keep = lax.dynamic_slice_in_dim(deconv_part, at["c"], 1, 1)[:, 0]
    deconv_sum = (keep.astype(F32) + shift(send, "c", 1).astype(F32)).astype(BF)
    deconv_sum = deconv_sum.reshape(4, 4, pad_dp, 3 * hidden)
    for dim, axis in enumerate(("y", "x")):
        total = lax.dynamic_slice_in_dim(deconv_sum, at[axis], 1, 0).astype(F32)
        for off in OFFSETS[1:]:
            block = lax.dynamic_slice_in_dim(deconv_sum, (at[axis] + off) % 4, 1, 0)
            total = total + shift(block, axis, off).astype(F32)
        deconv_sum = total[0] if axis == "x" else total[0].astype(BF)
    deconv_grad = jnp.transpose(deconv_sum[:rows_dp].reshape(rows_dp, 3, hidden), (1, 0, 2))

    scaled = feature_grad * gain
    stream_grad = inverse * (
        scaled
        - jnp.sum(scaled, axis=1, keepdims=True) / width
        - normed * (jnp.sum(scaled * normed, axis=1, keepdims=True) / width)
    ) * mask
    stream_bf = stream_grad.astype(BF)
    stream_pair = jnp.concatenate([stream_bf, shift(stream_bf, "c", 1)], axis=0)

    weight_part = dot(attn_cols, stream_pair, 0, 0).astype(BF)
    grad_parts = []
    for route, (lo, hi) in zip(ROUTES, CUTS):
        block = weight_part[:, lo:hi].reshape(4, 4, 4, LANE_ROWS, hi - lo)
        for axis in route[::-1]:
            block = scatter_axis(block, axis, ORDER.index(axis))
        grad_parts.append(block.reshape(LANE_ROWS, hi - lo))
    weight_grad = jnp.concatenate(grad_parts, axis=1).reshape(LANE_ROWS, groups, pad_dp)
    weight_grad = weight_grad[:own_rows, :, :rows_dp].reshape(own_rows, width)

    attn_part = dot(stream_pair, weight, 1, 1).astype(BF)
    other = shift(attn_part[tokens:], "c", 1)
    grad_attention = dot(attn_part[:tokens], pick_here, 1, 1) + dot(other, pick_there, 1, 1)

    grad_residual = stream_grad.reshape(tokens, groups, pad_dp)[:, :, :rows_dp].reshape(tokens, width)
    return (
        grad_residual[None],
        grad_attention.astype(BF)[None],
        weight_grad,
        deconv_grad,
        class_total,
    )


def solution(mesh):
    fine = Mesh(mesh.devices.reshape(4, 4, 2, 4), ("y", "x", "c", "z"))
    every = ("y", "x", "c", "z")
    batch = P(every, None, None)
    heads = P(None, ("y", "x", "c"), "z")
    in_specs = (batch, batch, P(every, None), P(), heads, P(), P(), P(), batch)
    out_specs = (batch, batch, P(every, None), heads, P())
    return jax.shard_map(
        per_device, mesh=fine, in_specs=in_specs, out_specs=out_specs, check_vma=False
    )
```

```python
import jax
import jax.numpy as jnp
from jax import lax
from jax.sharding import Mesh, PartitionSpec as P

BF = jnp.bfloat16
F32 = jnp.float32
OFFSETS = (0, 3, 1, 2)
LANE_ROWS = 16


def shift(value, axis, by):
    size = lax.axis_size(axis)
    return lax.ppermute(value, axis, [(i, (i + by) % size) for i in range(size)])


def gather_axis(piece, axis, dim):
    parts = [piece] + [shift(piece, axis, -off) for off in OFFSETS[1:]]
    return jnp.concatenate(parts, axis=dim)


def scatter_own(value, axis, index):
    total = lax.dynamic_index_in_dim(value, index, 0, keepdims=False).astype(F32)
    for off in OFFSETS[1:]:
        block = lax.dynamic_index_in_dim(value, (index + off) % 4, 0, keepdims=False)
        total = total + shift(block, axis, off).astype(F32)
    return total


def dot(a, b, ca, cb):
    return lax.dot_general(a, b, (((ca,), (cb,)), ((), ())), preferred_element_type=F32)


def silu_slope(values):
    sigmoid_value = jax.nn.sigmoid(values)
    return sigmoid_value * (1.0 + values * (1.0 - sigmoid_value))


def per_device(
    residual, attn_output, out_weight, norm_gain, head_deconv, classifier, labels, counts, cotangent
):
    at = {name: lax.axis_index(name) for name in ("y", "x", "c", "z")}
    samples = labels.shape[0]
    attention = attn_output[0]
    tokens, width = attention.shape
    hidden, classes = classifier.shape
    rows_dp = head_deconv.shape[1]
    pad_dp = 64
    groups = width // rows_dp
    wide = groups * pad_dp
    own_rows = out_weight.shape[0]

    padded = jnp.arange(wide)
    source = jnp.where(padded % pad_dp < rows_dp, padded // pad_dp * rows_dp + padded % pad_dp, -1)
    spread = (jnp.arange(width)[:, None] == source[None, :]).astype(BF)
    mask = (source >= 0).astype(F32)
    gain = jnp.pad(norm_gain.reshape(groups, rows_dp), ((0, 0), (0, pad_dp - rows_dp))).reshape(wide)

    piece = jnp.pad(dot(out_weight, spread, 1, 0).astype(BF), ((0, LANE_ROWS - own_rows), (0, 0)))
    weight = lax.all_gather(piece, ("y", "x", "z"), axis=0, tiled=True)

    heads_local = jnp.pad(
        jnp.transpose(head_deconv, (1, 0, 2)).reshape(rows_dp, -1), ((0, pad_dp - rows_dp), (0, 0))
    )
    heads = lax.all_gather(heads_local, ("y", "x", "c"), axis=0, tiled=True)

    row = jnp.arange(64 * LANE_ROWS)
    sub = row % LANE_ROWS
    ring = row // LANE_ROWS

    def select_for(core):
        target = ((ring // 4 * 2 + core) * 4 + ring % 4) * own_rows + sub
        target = jnp.where(sub < own_rows, target, -1)
        return (jnp.arange(width)[:, None] == target[None, :]).astype(BF)

    pick_here = select_for(at["c"])
    pick_there = select_for(1 - at["c"])
    attn_pair = jnp.concatenate([attention, shift(attention, "c", 1)], axis=0)
    attn_cols = dot(attn_pair, pick_here, 1, 0).astype(BF)
    attn_ring = gather_axis(attn_cols, "z", 0)
    residual_wide = dot(residual[0], spread, 1, 0)

    cot_blocks = []
    label_rows = []
    for off in OFFSETS:
        cut = lax.dynamic_slice_in_dim(cotangent[0], ((at["z"] - off) % 4) * classes, classes, 1)
        cot_blocks.append(cut if off == 0 else shift(cut, "z", -off))
        index = ((at["y"] * 4 + at["x"]) * 2 + at["c"]) * 4 + (at["z"] + off) % 4
        label_rows.append(lax.dynamic_slice_in_dim(labels, index, 1, 0))
    task_weight = samples / (3.0 * counts.astype(F32))
    column = jnp.arange(classes)
    column_task = (column >= 1).astype(jnp.int32) + (column >= 4).astype(jnp.int32)
    column_hot = (column_task[None, :] == jnp.arange(3)[:, None]).astype(F32)
    column_weight = jnp.sum(column_hot * task_weight[:, None], axis=0)
    label_mask = jnp.sum(
        jnp.concatenate(label_rows, 0).astype(F32)[:, :, None] * column_hot[None], axis=1
    )
    pred_grad = (
        jnp.stack(cot_blocks).astype(F32) * (label_mask * column_weight[None, :])[:, None, :]
    ).astype(BF).reshape(4 * tokens, classes)
    class_wide = (
        jnp.transpose(classifier).astype(F32)[:, None, :] * jnp.transpose(column_hot)[:, :, None]
    ).astype(BF).reshape(classes, 3 * hidden)

    product = dot(attn_cols, weight, 1, 0)
    stream = residual_wide + product[:tokens] + shift(product[tokens:].astype(BF), "c", 1).astype(F32)
    center = (stream - jnp.sum(stream, axis=1, keepdims=True) / width) * mask
    inverse = lax.rsqrt(jnp.sum(center * center, axis=1, keepdims=True) / width + 1e-06)
    normed = center * inverse
    features = (normed * gain).astype(BF)
    blocks = [features] + [shift(features, "z", -off) for off in OFFSETS[1:]]
    grads, activations, returned = [], [], []
    for first, last in ((0, 1), (1, 3), (3, 4)):
        feats = jnp.concatenate(blocks[first:last], axis=0)
        pre_act = dot(feats, heads, 1, 0)
        act_grad = dot(pred_grad[first * tokens : last * tokens], class_wide, 1, 0)
        activations.append(jax.nn.silu(pre_act).astype(BF))
        grads.append((act_grad * silu_slope(pre_act)).astype(BF))
        back = dot(grads[-1], heads, 1, 1)
        for digit in range(first, last):
            part = back[(digit - first) * tokens : (digit - first + 1) * tokens]
            if digit:
                part = shift(part.astype(BF), "z", OFFSETS[digit])
            returned.append(part)
    feats = jnp.concatenate(blocks, axis=0)
    pre_grad = jnp.concatenate(grads, axis=0)

    class_part = dot(pred_grad, jnp.concatenate(activations, axis=0), 0, 0)
    class_part = class_part.reshape(classes, 3, hidden) * jnp.transpose(column_hot)[:, :, None]
    class_rows = jnp.pad(
        jnp.sum(class_part, axis=1)[:, None, :],
        ((0, 0), (rows_dp, pad_dp - rows_dp - 1), (0, 2 * hidden)),
    )
    deconv_part = dot(feats, pre_grad, 0, 0).reshape(groups, pad_dp, 3 * hidden) + class_rows
    deconv_part = deconv_part.astype(BF).reshape(groups // 2, 2, pad_dp, 3 * hidden)
    send = lax.dynamic_slice_in_dim(deconv_part, 1 - at["c"], 1, 1)[:, 0]
    keep = lax.dynamic_slice_in_dim(deconv_part, at["c"], 1, 1)[:, 0]
    deconv_sum = (keep.astype(F32) + shift(send, "c", 1).astype(F32)).astype(BF)
    held = lax.optimization_barrier((deconv_sum, *returned))
    deconv_sum, returned = held[0], held[1:]
    feature_grad = sum(part.astype(F32) for part in returned)

    deconv_sum = scatter_own(deconv_sum.reshape(4, 4, pad_dp, 3 * hidden), "y", at["y"]).astype(BF)
    deconv_sum = scatter_own(deconv_sum, "x", at["x"])
    deconv_grad = jnp.transpose(deconv_sum[:rows_dp].reshape(rows_dp, 3, hidden), (1, 0, 2))
    class_all = lax.all_gather(
        deconv_sum[rows_dp : rows_dp + 1, :hidden], ("y", "x", "c", "z"), axis=0, tiled=True
    )
    class_total = jnp.transpose(jnp.sum(class_all.reshape(classes, 4, hidden), axis=1))

    scaled = feature_grad * gain
    stream_grad = inverse * (
        scaled
        - jnp.sum(scaled, axis=1, keepdims=True) / width
        - normed * (jnp.sum(scaled * normed, axis=1, keepdims=True) / width)
    ) * mask
    stream_bf = stream_grad.astype(BF)
    cols = wide // 4
    slabs = []
    for off in OFFSETS:
        slab = lax.dynamic_slice_in_dim(stream_bf, ((at["z"] - off) % 4) * cols, cols, 1)
        slabs.append(slab if off == 0 else shift(slab, "z", -off))
    slab = jnp.stack(slabs)
    stream_ring = jnp.stack([slab, shift(slab, "c", 1)], axis=1).reshape(8 * tokens, cols)
    weight_part = dot(attn_ring, stream_ring, 0, 0).astype(BF).reshape(4, 4, 4 * LANE_ROWS, cols)
    weight_part = scatter_own(weight_part, "y", at["y"]).astype(BF)
    weight_part = scatter_own(weight_part, "x", at["x"]).reshape(4, LANE_ROWS, cols)
    ordered = jnp.zeros((4, LANE_ROWS, cols), F32)
    for off in OFFSETS:
        strip = lax.dynamic_index_in_dim(weight_part, (at["z"] - off) % 4, 0)
        if off:
            strip = shift(strip, "z", -off)
        ordered = lax.dynamic_update_slice_in_dim(ordered, strip, (at["z"] + off) % 4, 0)
    weight_grad = jnp.transpose(ordered, (1, 0, 2)).reshape(LANE_ROWS, groups, pad_dp)
    weight_grad = weight_grad[:own_rows, :, :rows_dp].reshape(own_rows, width)

    stream_pair = jnp.concatenate([stream_bf, shift(stream_bf, "c", 1)], axis=0)
    attn_part = dot(stream_pair, weight, 1, 1).astype(BF)
    other = shift(attn_part[tokens:], "c", 1)
    grad_attention = dot(attn_part[:tokens], pick_here, 1, 1) + dot(other, pick_there, 1, 1)

    grad_residual = stream_grad.reshape(tokens, groups, pad_dp)[:, :, :rows_dp].reshape(tokens, width)
    return (
        grad_residual[None],
        grad_attention.astype(BF)[None],
        weight_grad,
        deconv_grad,
        class_total,
    )


def solution(mesh):
    fine = Mesh(mesh.devices.reshape(4, 4, 2, 4), ("y", "x", "c", "z"))
    every = ("y", "x", "c", "z")
    batch = P(every, None, None)
    heads = P(None, ("y", "x", "c"), "z")
    in_specs = (batch, batch, P(every, None), P(), heads, P(), P(), P(), batch)
    out_specs = (batch, batch, P(every, None), heads, P())
    return jax.shard_map(
        per_device, mesh=fine, in_specs=in_specs, out_specs=out_specs, check_vma=False
    )
```

```python
import jax
import jax.numpy as jnp
from jax import lax
from jax.sharding import Mesh, PartitionSpec as P

BF = jnp.bfloat16
F32 = jnp.float32
OFFSETS = (0, 3, 1, 2)
LANE_ROWS = 16


def shift(value, axis, by):
    size = lax.axis_size(axis)
    return lax.ppermute(value, axis, [(i, (i + by) % size) for i in range(size)])


def gather_axis(piece, axis, dim):
    parts = [piece] + [shift(piece, axis, -off) for off in OFFSETS[1:]]
    return jnp.concatenate(parts, axis=dim)


def scatter_axis(value, axis):
    total = value[0]
    for digit, off in enumerate(OFFSETS[1:], 1):
        total = total + shift(value[digit].astype(BF), axis, off).astype(F32)
    return total


def scatter_own(value, axis, index):
    total = lax.dynamic_index_in_dim(value, index, 0, keepdims=False).astype(F32)
    for off in OFFSETS[1:]:
        block = lax.dynamic_index_in_dim(value, (index + off) % 4, 0, keepdims=False)
        total = total + shift(block, axis, off).astype(F32)
    return total


def dot(a, b, ca, cb):
    return lax.dot_general(a, b, (((ca,), (cb,)), ((), ())), preferred_element_type=F32)


def silu_slope(values):
    sigmoid_value = jax.nn.sigmoid(values)
    return sigmoid_value * (1.0 + values * (1.0 - sigmoid_value))


def per_device(
    residual, attn_output, out_weight, norm_gain, head_deconv, classifier, labels, counts, cotangent
):
    at = {name: lax.axis_index(name) for name in ("y", "x", "c", "z")}
    samples = labels.shape[0]
    attention = attn_output[0]
    tokens, width = attention.shape
    hidden, classes = classifier.shape
    rows_dp = head_deconv.shape[1]
    pad_dp = 64
    groups = width // rows_dp
    wide = groups * pad_dp
    own_rows = out_weight.shape[0]

    padded = jnp.arange(wide)
    source = jnp.where(padded % pad_dp < rows_dp, padded // pad_dp * rows_dp + padded % pad_dp, -1)
    spread = (jnp.arange(width)[:, None] == source[None, :]).astype(BF)
    mask = (source >= 0).astype(F32)
    gain = jnp.pad(norm_gain.reshape(groups, rows_dp), ((0, 0), (0, pad_dp - rows_dp))).reshape(wide)

    piece = jnp.pad(dot(out_weight, spread, 1, 0).astype(BF), ((0, LANE_ROWS - own_rows), (0, 0)))
    cols = wide // 4
    strips = jnp.zeros((4, LANE_ROWS, cols), BF)
    for off in OFFSETS:
        strip = lax.dynamic_slice_in_dim(piece, ((at["z"] - off) % 4) * cols, cols, 1)
        if off:
            strip = shift(strip, "z", -off)
        strips = lax.dynamic_update_slice_in_dim(strips, strip[None], (at["z"] + off) % 4, 0)
    weight = strips.reshape(4 * LANE_ROWS, cols)
    weight = gather_axis(gather_axis(weight, "y", 0), "x", 0)
    weight = jnp.concatenate([weight, shift(weight, "c", 1)], axis=0)

    heads_local = jnp.pad(
        jnp.transpose(head_deconv, (1, 0, 2)).reshape(rows_dp, -1), ((0, pad_dp - rows_dp), (0, 0))
    )
    heads = lax.all_gather(heads_local, ("y", "x", "c"), axis=0, tiled=True)

    table = jnp.array(OFFSETS, jnp.int32)
    row = jnp.arange(128 * LANE_ROWS)
    sub = row % LANE_ROWS
    row_y = (at["y"] + table[row // (4 * LANE_ROWS) % 4]) % 4
    row_x = (at["x"] + table[row // (16 * LANE_ROWS) % 4]) % 4
    row_c = (at["c"] + row // (64 * LANE_ROWS)) % 2
    target = (((row_y * 4 + row_x) * 2 + row_c) * 4 + row // LANE_ROWS % 4) * own_rows + sub
    target = jnp.where(sub < own_rows, target, -1)
    pick = (jnp.arange(width)[:, None] == target[None, :]).astype(BF)
    attn_ring = gather_axis(dot(attention, pick, 1, 0).astype(BF), "z", 0)
    residual_wide = dot(residual[0], spread, 1, 0)

    cot_blocks = []
    label_rows = []
    for off in OFFSETS:
        cut = lax.dynamic_slice_in_dim(cotangent[0], ((at["z"] - off) % 4) * classes, classes, 1)
        cot_blocks.append(cut if off == 0 else shift(cut, "z", -off))
        index = ((at["y"] * 4 + at["x"]) * 2 + at["c"]) * 4 + (at["z"] + off) % 4
        label_rows.append(lax.dynamic_slice_in_dim(labels, index, 1, 0))
    task_weight = samples / (3.0 * counts.astype(F32))
    column = jnp.arange(classes)
    column_task = (column >= 1).astype(jnp.int32) + (column >= 4).astype(jnp.int32)
    column_hot = (column_task[None, :] == jnp.arange(3)[:, None]).astype(F32)
    column_weight = jnp.sum(column_hot * task_weight[:, None], axis=0)
    label_mask = jnp.sum(
        jnp.concatenate(label_rows, 0).astype(F32)[:, :, None] * column_hot[None], axis=1
    )
    pred_grad = (
        jnp.stack(cot_blocks).astype(F32) * (label_mask * column_weight[None, :])[:, None, :]
    ).astype(BF).reshape(4 * tokens, classes)
    class_wide = (
        jnp.transpose(classifier).astype(F32)[:, None, :] * jnp.transpose(column_hot)[:, :, None]
    ).astype(BF).reshape(classes, 3 * hidden)

    product, late = lax.optimization_barrier((dot(attn_ring, weight, 1, 0), piece))
    parts = []
    for digit, off in enumerate(OFFSETS):
        part = product[digit * tokens : (digit + 1) * tokens]
        parts.append(shift(part.astype(BF), "z", off).astype(F32) if off else part)
    parts = jnp.stack(parts)
    places = jnp.array([0, 2, 3, 1], jnp.int32)
    projected = jnp.concatenate(
        [lax.dynamic_index_in_dim(parts, places[(at["z"] - i) % 4], 0, False) for i in range(4)], 1
    )
    stream = residual_wide + projected
    center = (stream - jnp.sum(stream, axis=1, keepdims=True) / width) * mask
    inverse = lax.rsqrt(jnp.sum(center * center, axis=1, keepdims=True) / width + 1e-06)
    normed = center * inverse
    features = (normed * gain).astype(BF)
    blocks = [features] + [shift(features, "z", -off) for off in OFFSETS[1:]]
    grads, activations, returned = [], [], []
    for first, last in ((0, 1), (1, 3), (3, 4)):
        feats = jnp.concatenate(blocks[first:last], axis=0)
        pre_act = dot(feats, heads, 1, 0)
        act_grad = dot(pred_grad[first * tokens : last * tokens], class_wide, 1, 0)
        activations.append(jax.nn.silu(pre_act).astype(BF))
        grads.append((act_grad * silu_slope(pre_act)).astype(BF))
        back = dot(grads[-1], heads, 1, 1)
        for digit in range(first, last):
            part = back[(digit - first) * tokens : (digit - first + 1) * tokens]
            if digit:
                part = shift(part.astype(BF), "z", OFFSETS[digit])
            returned.append(part)
    feats = jnp.concatenate(blocks, axis=0)
    pre_grad = jnp.concatenate(grads, axis=0)

    class_part = dot(pred_grad, jnp.concatenate(activations, axis=0), 0, 0)
    class_part = class_part.reshape(classes, 3, hidden) * jnp.transpose(column_hot)[:, :, None]
    class_rows = jnp.pad(
        jnp.sum(class_part, axis=1)[:, None, :],
        ((0, 0), (rows_dp, pad_dp - rows_dp - 1), (0, 2 * hidden)),
    )
    deconv_part = dot(feats, pre_grad, 0, 0).reshape(groups, pad_dp, 3 * hidden) + class_rows
    deconv_part = deconv_part.astype(BF).reshape(groups // 2, 2, pad_dp, 3 * hidden)
    send = lax.dynamic_slice_in_dim(deconv_part, 1 - at["c"], 1, 1)[:, 0]
    keep = lax.dynamic_slice_in_dim(deconv_part, at["c"], 1, 1)[:, 0]
    deconv_sum = (keep.astype(F32) + shift(send, "c", 1).astype(F32)).astype(BF)
    held = lax.optimization_barrier((deconv_sum, *returned))
    deconv_sum, returned = held[0], held[1:]
    feature_grad = sum(part.astype(F32) for part in returned)
    deconv_sum = scatter_own(deconv_sum.reshape(4, 4, pad_dp, 3 * hidden), "y", at["y"]).astype(BF)

    scaled = feature_grad * gain
    stream_grad = inverse * (
        scaled
        - jnp.sum(scaled, axis=1, keepdims=True) / width
        - normed * (jnp.sum(scaled * normed, axis=1, keepdims=True) / width)
    ) * mask
    stream_bf, deconv_sum = lax.optimization_barrier((stream_grad.astype(BF), deconv_sum))

    slabs = []
    for off in OFFSETS:
        slab = lax.dynamic_slice_in_dim(stream_bf, ((at["z"] - off) % 4) * cols, cols, 1)
        slabs.append(slab if off == 0 else shift(slab, "z", -off))
    weight_part = dot(attn_ring, jnp.concatenate(slabs, axis=0), 0, 0)
    half = 64 * LANE_ROWS
    weight_part = weight_part[:half] + shift(weight_part[half:].astype(BF), "c", 1).astype(F32)
    weight_part = scatter_axis(weight_part.reshape(4, 4, 4, LANE_ROWS, cols), "x")
    weight_part = scatter_axis(weight_part, "y")
    ordered = jnp.zeros((4, LANE_ROWS, cols), F32)
    for off in OFFSETS:
        strip = lax.dynamic_index_in_dim(weight_part, (at["z"] - off) % 4, 0)
        if off:
            strip = shift(strip, "z", -off)
        ordered = lax.dynamic_update_slice_in_dim(ordered, strip, (at["z"] + off) % 4, 0)
    weight_grad = jnp.transpose(ordered, (1, 0, 2)).reshape(LANE_ROWS, groups, pad_dp)
    weight_grad = weight_grad[:own_rows, :, :rows_dp].reshape(own_rows, width)

    deconv_sum = scatter_own(deconv_sum, "x", at["x"])
    deconv_grad = jnp.transpose(deconv_sum[:rows_dp].reshape(rows_dp, 3, hidden), (1, 0, 2))
    class_total = jnp.zeros((classes, hidden), F32)
    index_dp = (at["y"] * 4 + at["x"]) * 2 + at["c"]
    class_total = lax.dynamic_update_slice_in_dim(
        class_total, deconv_sum[rows_dp : rows_dp + 1, :hidden], index_dp, 0
    )
    for axis in ("x", "y", "z"):
        class_total = sum([shift(class_total, axis, off) for off in OFFSETS[1:]], class_total)
    class_total = jnp.transpose(class_total + shift(class_total, "c", 1))

    whole = lax.all_gather(late, ("y", "x", "c", "z"), axis=0, tiled=True)
    natural = jnp.arange(128 * LANE_ROWS)
    natural = jnp.where(
        natural % LANE_ROWS < own_rows, natural // LANE_ROWS * own_rows + natural % LANE_ROWS, -1
    )
    unpick = (natural[:, None] == jnp.arange(width)[None, :]).astype(BF)
    grad_attention = dot(dot(stream_bf, whole, 1, 1).astype(BF), unpick, 1, 0)

    grad_residual = stream_grad.reshape(tokens, groups, pad_dp)[:, :, :rows_dp].reshape(tokens, width)
    return (
        grad_residual[None],
        grad_attention.astype(BF)[None],
        weight_grad,
        deconv_grad,
        class_total,
    )


def solution(mesh):
    fine = Mesh(mesh.devices.reshape(4, 4, 2, 4), ("y", "x", "c", "z"))
    every = ("y", "x", "c", "z")
    batch = P(every, None, None)
    heads = P(None, ("y", "x", "c"), "z")
    in_specs = (batch, batch, P(every, None), P(), heads, P(), P(), P(), batch)
    out_specs = (batch, batch, P(every, None), heads, P())
    return jax.shard_map(
        per_device, mesh=fine, in_specs=in_specs, out_specs=out_specs, check_vma=False
    )
```

```python
import jax
import jax.numpy as jnp
from jax import lax
from jax.sharding import Mesh, PartitionSpec as P

BF = jnp.bfloat16
F32 = jnp.float32
OFFSETS = (0, 3, 1, 2)
LANE_ROWS = 16


def shift(value, axis, by):
    size = lax.axis_size(axis)
    return lax.ppermute(value, axis, [(i, (i + by) % size) for i in range(size)])


def exchange(value, axis, bit):
    return lax.ppermute(value, axis, [(i, i ^ bit) for i in range(lax.axis_size(axis))])


def gather_axis(piece, axis, dim):
    parts = [piece] + [shift(piece, axis, -off) for off in OFFSETS[1:]]
    return jnp.concatenate(parts, axis=dim)


def scatter_axis(value, axis):
    total = value[0]
    for digit, off in enumerate(OFFSETS[1:], 1):
        total = total + shift(value[digit].astype(BF), axis, off).astype(F32)
    return total


def scatter_own(value, axis, index):
    total = lax.dynamic_index_in_dim(value, index, 0, keepdims=False).astype(F32)
    for off in OFFSETS[1:]:
        block = lax.dynamic_index_in_dim(value, (index + off) % 4, 0, keepdims=False)
        total = total + shift(block, axis, off).astype(F32)
    return total


def dot(a, b, ca, cb):
    return lax.dot_general(a, b, (((ca,), (cb,)), ((), ())), preferred_element_type=F32)


def silu_slope(values):
    sigmoid_value = jax.nn.sigmoid(values)
    return sigmoid_value * (1.0 + values * (1.0 - sigmoid_value))


def per_device(
    residual, attn_output, out_weight, norm_gain, head_deconv, classifier, labels, counts, cotangent
):
    at = {name: lax.axis_index(name) for name in ("y", "x", "c", "z")}
    samples = labels.shape[0]
    attention = attn_output[0]
    tokens, width = attention.shape
    hidden, classes = classifier.shape
    rows_dp = head_deconv.shape[1]
    pad_dp = 64
    groups = width // rows_dp
    wide = groups * pad_dp
    own_rows = out_weight.shape[0]

    padded = jnp.arange(wide)
    source = jnp.where(padded % pad_dp < rows_dp, padded // pad_dp * rows_dp + padded % pad_dp, -1)
    spread = (jnp.arange(width)[:, None] == source[None, :]).astype(BF)
    mask = (source >= 0).astype(F32)
    gain = jnp.pad(norm_gain.reshape(groups, rows_dp), ((0, 0), (0, pad_dp - rows_dp))).reshape(wide)

    piece = jnp.pad(dot(out_weight, spread, 1, 0).astype(BF), ((0, LANE_ROWS - own_rows), (0, 0)))
    cols = wide // 4
    strips = jnp.zeros((4, LANE_ROWS, cols), BF)
    for off in OFFSETS:
        strip = lax.dynamic_slice_in_dim(piece, ((at["z"] - off) % 4) * cols, cols, 1)
        if off:
            strip = shift(strip, "z", -off)
        strips = lax.dynamic_update_slice_in_dim(strips, strip[None], (at["z"] + off) % 4, 0)

    heads_local = jnp.pad(
        jnp.transpose(head_deconv, (1, 0, 2)).reshape(rows_dp, -1), ((0, pad_dp - rows_dp), (0, 0))
    )
    heads = lax.all_gather(heads_local, ("y", "x", "c"), axis=0, tiled=True)

    table = jnp.array(OFFSETS, jnp.int32)
    row = jnp.arange(128 * LANE_ROWS)
    sub = row % LANE_ROWS
    row_y = (at["y"] + table[row // (4 * LANE_ROWS) % 4]) % 4
    row_x = (at["x"] + table[row // (16 * LANE_ROWS) % 4]) % 4
    row_c = (at["c"] + row // (64 * LANE_ROWS)) % 2
    target = (((row_y * 4 + row_x) * 2 + row_c) * 4 + row // LANE_ROWS % 4) * own_rows + sub
    target = jnp.where(sub < own_rows, target, -1)
    pick = (jnp.arange(width)[:, None] == target[None, :]).astype(BF)
    attn_own, weight = lax.optimization_barrier(
        (dot(attention, pick, 1, 0).astype(BF), strips.reshape(4 * LANE_ROWS, cols))
    )
    attn_ring = gather_axis(attn_own, "z", 0)
    weight = gather_axis(gather_axis(weight, "y", 0), "x", 0)
    weight = jnp.concatenate([weight, shift(weight, "c", 1)], axis=0)
    residual_wide = dot(residual[0], spread, 1, 0)

    cot_blocks = []
    label_rows = []
    for off in OFFSETS:
        cut = lax.dynamic_slice_in_dim(cotangent[0], ((at["z"] - off) % 4) * classes, classes, 1)
        cot_blocks.append(cut if off == 0 else shift(cut, "z", -off))
        index = ((at["y"] * 4 + at["x"]) * 2 + at["c"]) * 4 + (at["z"] + off) % 4
        label_rows.append(lax.dynamic_slice_in_dim(labels, index, 1, 0))
    task_weight = samples / (3.0 * counts.astype(F32))
    column = jnp.arange(classes)
    column_task = (column >= 1).astype(jnp.int32) + (column >= 4).astype(jnp.int32)
    column_hot = (column_task[None, :] == jnp.arange(3)[:, None]).astype(F32)
    column_weight = jnp.sum(column_hot * task_weight[:, None], axis=0)
    label_mask = jnp.sum(
        jnp.concatenate(label_rows, 0).astype(F32)[:, :, None] * column_hot[None], axis=1
    )
    pred_grad = (
        jnp.stack(cot_blocks).astype(F32) * (label_mask * column_weight[None, :])[:, None, :]
    ).astype(BF).reshape(4 * tokens, classes)
    class_wide = (
        jnp.transpose(classifier).astype(F32)[:, None, :] * jnp.transpose(column_hot)[:, :, None]
    ).astype(BF).reshape(classes, 3 * hidden)

    weight, pred_grad, class_wide, gain, residual_wide = lax.optimization_barrier(
        (weight, pred_grad, class_wide, gain, residual_wide)
    )
    product = dot(attn_ring, weight, 1, 0)
    parts = []
    for digit, off in enumerate(OFFSETS):
        part = product[digit * tokens : (digit + 1) * tokens]
        parts.append(shift(part.astype(BF), "z", off).astype(F32) if off else part)
    parts = jnp.stack(parts)
    places = jnp.array([0, 2, 3, 1], jnp.int32)
    projected = jnp.concatenate(
        [lax.dynamic_index_in_dim(parts, places[(at["z"] - i) % 4], 0, False) for i in range(4)], 1
    )
    stream = residual_wide + projected
    center = (stream - jnp.sum(stream, axis=1, keepdims=True) / width) * mask
    inverse = lax.rsqrt(jnp.sum(center * center, axis=1, keepdims=True) / width + 1e-06)
    normed = center * inverse
    features = (normed * gain).astype(BF)
    blocks = [features] + [shift(features, "z", -off) for off in OFFSETS[1:]]
    grads, activations, returned = [], [], []
    for first, last in ((0, 1), (1, 3), (3, 4)):
        feats = jnp.concatenate(blocks[first:last], axis=0)
        pre_act = dot(feats, heads, 1, 0)
        act_grad = dot(pred_grad[first * tokens : last * tokens], class_wide, 1, 0)
        activations.append(jax.nn.silu(pre_act).astype(BF))
        grads.append((act_grad * silu_slope(pre_act)).astype(BF))
        back = dot(grads[-1], heads, 1, 1)
        for digit in range(first, last):
            part = back[(digit - first) * tokens : (digit - first + 1) * tokens]
            if digit:
                part = shift(part.astype(BF), "z", OFFSETS[digit])
            returned.append(part)
    feats = jnp.concatenate(blocks, axis=0)
    pre_grad = jnp.concatenate(grads, axis=0)

    class_part = dot(pred_grad, jnp.concatenate(activations, axis=0), 0, 0)
    class_part = class_part.reshape(classes, 3, hidden) * jnp.transpose(column_hot)[:, :, None]
    class_total = jnp.sum(class_part, axis=1)
    for axis, bit in (("c", 1), ("z", 1), ("z", 2), ("x", 1), ("x", 2), ("y", 1), ("y", 2)):
        class_total = class_total + exchange(class_total, axis, bit)
    deconv_part = dot(feats, pre_grad, 0, 0).astype(BF)
    deconv_part = deconv_part.reshape(groups // 2, 2, pad_dp, 3 * hidden)
    send = lax.dynamic_slice_in_dim(deconv_part, 1 - at["c"], 1, 1)[:, 0]
    keep = lax.dynamic_slice_in_dim(deconv_part, at["c"], 1, 1)[:, 0]
    deconv_sum = (keep.astype(F32) + shift(send, "c", 1).astype(F32)).astype(BF)
    deconv_sum, returned[1] = lax.optimization_barrier((deconv_sum, returned[1]))
    feature_grad = sum(part.astype(F32) for part in returned)
    deconv_sum = scatter_own(deconv_sum.reshape(4, 4, pad_dp, 3 * hidden), "y", at["y"]).astype(BF)

    scaled = feature_grad * gain
    stream_grad = inverse * (
        scaled
        - jnp.sum(scaled, axis=1, keepdims=True) / width
        - normed * (jnp.sum(scaled * normed, axis=1, keepdims=True) / width)
    ) * mask
    stream_bf = stream_grad.astype(BF)

    slabs = []
    for off in OFFSETS:
        slab = lax.dynamic_slice_in_dim(stream_bf, ((at["z"] - off) % 4) * cols, cols, 1)
        slabs.append(slab if off == 0 else shift(slab, "z", -off))
    stream_ring = jnp.concatenate(slabs, axis=0)
    weight_part = dot(attn_ring, stream_ring, 0, 0)
    half = 64 * LANE_ROWS
    weight_part = weight_part[:half] + shift(weight_part[half:].astype(BF), "c", 1).astype(F32)
    weight_part = scatter_axis(weight_part.reshape(4, 4, 4, LANE_ROWS, cols), "x")
    weight_part = scatter_axis(weight_part, "y")
    ordered = jnp.zeros((4, LANE_ROWS, cols), F32)
    for off in OFFSETS:
        strip = lax.dynamic_index_in_dim(weight_part, (at["z"] - off) % 4, 0)
        if off:
            strip = shift(strip, "z", -off)
        ordered = lax.dynamic_update_slice_in_dim(ordered, strip, (at["z"] + off) % 4, 0)
    weight_grad = jnp.transpose(ordered, (1, 0, 2)).reshape(LANE_ROWS, groups, pad_dp)
    weight_grad = weight_grad[:own_rows, :, :rows_dp].reshape(own_rows, width)

    deconv_sum = scatter_own(deconv_sum, "x", at["x"])
    deconv_grad = jnp.transpose(deconv_sum[:rows_dp].reshape(rows_dp, 3, hidden), (1, 0, 2))

    attn_part = dot(stream_ring, weight, 1, 1).reshape(4, tokens, 128 * LANE_ROWS)
    grad_attention = dot(scatter_axis(attn_part, "z").astype(BF), pick, 1, 1)

    grad_residual = stream_grad.reshape(tokens, groups, pad_dp)[:, :, :rows_dp].reshape(tokens, width)
    return (
        grad_residual[None],
        grad_attention.astype(BF)[None],
        weight_grad,
        deconv_grad,
        jnp.transpose(class_total),
    )


def solution(mesh):
    fine = Mesh(mesh.devices.reshape(4, 4, 2, 4), ("y", "x", "c", "z"))
    every = ("y", "x", "c", "z")
    batch = P(every, None, None)
    heads = P(None, ("y", "x", "c"), "z")
    in_specs = (batch, batch, P(every, None), P(), heads, P(), P(), P(), batch)
    out_specs = (batch, batch, P(every, None), heads, P())
    return jax.shard_map(
        per_device, mesh=fine, in_specs=in_specs, out_specs=out_specs, check_vma=False
    )
```

```python
import jax
import jax.numpy as jnp
from jax import lax
from jax.sharding import Mesh, PartitionSpec as P

BF = jnp.bfloat16
F32 = jnp.float32
OFFSETS = (0, 3, 1, 2)
LANE_ROWS = 16


def shift(value, axis, by):
    size = lax.axis_size(axis)
    return lax.ppermute(value, axis, [(i, (i + by) % size) for i in range(size)])


def exchange(value, axis, bit):
    return lax.ppermute(value, axis, [(i, i ^ bit) for i in range(lax.axis_size(axis))])


def gather_axis(piece, axis, dim):
    parts = [piece] + [shift(piece, axis, -off) for off in OFFSETS[1:]]
    return jnp.concatenate(parts, axis=dim)


def scatter_axis(value, axis):
    total = value[0]
    for digit, off in enumerate(OFFSETS[1:], 1):
        total = total + shift(value[digit].astype(BF), axis, off).astype(F32)
    return total


def collect(blocks, axis):
    total = blocks[0]
    for digit, off in enumerate(OFFSETS[1:], 1):
        total = total + shift(blocks[digit], axis, off).astype(F32)
    return total


def quarter(value):
    blocks = jnp.split(value, 4, axis=0)
    return [blocks[0]] + [block.astype(BF) for block in blocks[1:]]


def halves(value, low):
    first, second = jnp.split(value, 2, axis=0)
    return jnp.where(low, first, second), jnp.where(low, second, first).astype(BF)


def halve(value, axis, bit, index):
    mine, theirs = halves(value, index // bit % 2 == 0)
    return mine + exchange(theirs, axis, bit).astype(F32)


def dot(a, b, ca, cb):
    return lax.dot_general(a, b, (((ca,), (cb,)), ((), ())), preferred_element_type=F32)


def stage(*values):
    return lax.optimization_barrier(values)


def silu_slope(values):
    sigmoid_value = jax.nn.sigmoid(values)
    return sigmoid_value * (1.0 + values * (1.0 - sigmoid_value))


def per_device(
    residual, attn_output, out_weight, norm_gain, head_deconv, classifier, labels, counts, cotangent
):
    at = {name: lax.axis_index(name) for name in ("y", "x", "c", "z")}
    samples = labels.shape[0]
    attention = attn_output[0]
    tokens, width = attention.shape
    hidden, classes = classifier.shape
    rows_dp = head_deconv.shape[1]
    pad_dp = 64
    groups = width // rows_dp
    wide = groups * pad_dp
    half = wide // 2
    cols = wide // 4
    own_rows = out_weight.shape[0]

    padded = jnp.arange(wide)
    place = (padded // pad_dp % (groups // 2) * 2 + padded // half) * rows_dp + padded % pad_dp
    source = jnp.where(padded % pad_dp < rows_dp, place, -1)
    spread = (jnp.arange(width)[:, None] == source[None, :]).astype(BF)
    mask = (source >= 0).astype(F32)
    gain = jnp.transpose(norm_gain.reshape(groups // 2, 2, rows_dp), (1, 0, 2))
    gain = jnp.pad(gain, ((0, 0), (0, 0), (0, pad_dp - rows_dp))).reshape(wide)

    heads_local = jnp.pad(
        jnp.transpose(head_deconv, (1, 0, 2)).reshape(rows_dp, -1), ((0, pad_dp - rows_dp), (0, 0))
    )
    heads = lax.all_gather(heads_local, ("c", "y", "x"), axis=0, tiled=True)

    table = jnp.array(OFFSETS, jnp.int32)
    row = jnp.arange(128 * LANE_ROWS)
    sub = row % LANE_ROWS
    row_y = (at["y"] + table[row // (4 * LANE_ROWS) % 4]) % 4
    row_x = (at["x"] + table[row // (16 * LANE_ROWS) % 4]) % 4
    row_c = (at["c"] + row // (64 * LANE_ROWS)) % 2
    target = (((row_y * 4 + row_x) * 2 + row_c) * 4 + row // LANE_ROWS % 4) * own_rows + sub
    target = jnp.where(sub < own_rows, target, -1)
    pick = (jnp.arange(width)[:, None] == target[None, :]).astype(BF)

    natural = jnp.arange(128 * LANE_ROWS)
    natural = jnp.where(
        natural % LANE_ROWS < own_rows, natural // LANE_ROWS * own_rows + natural % LANE_ROWS, -1
    )
    unpick = (natural[:, None] == jnp.arange(width)[None, :]).astype(BF)

    piece = jnp.pad(dot(out_weight, spread, 1, 0).astype(BF), ((0, LANE_ROWS - own_rows), (0, 0)))
    attn_blocks = [dot(attention, pick, 1, 0).astype(BF)]
    piece, attn_blocks[0] = stage(piece, attn_blocks[0])
    weight = jnp.zeros((4, LANE_ROWS, cols), BF)
    for off in OFFSETS:
        strip = lax.dynamic_slice_in_dim(piece, ((at["z"] - off) % 4) * cols, cols, 1)
        if off:
            strip = shift(strip, "z", -off)
        weight = lax.dynamic_update_slice_in_dim(weight, strip[None], (at["z"] + off) % 4, 0)
    weight = weight.reshape(4 * LANE_ROWS, cols)
    for digit, axis in ((1, "y"), (2, "x"), (3, "c")):
        attn_blocks.append(shift(attn_blocks[0], "z", -OFFSETS[digit]))
        weight, attn_blocks = stage(weight, attn_blocks)
        if axis != "c":
            weight = gather_axis(weight, axis, 0)
    weight_there = exchange(weight, "c", 1)
    product = [dot(block[:, :half], weight, 1, 0) for block in attn_blocks]
    residual_wide = dot(residual[0], spread, 1, 0)

    cot_blocks = []
    label_rows = []
    for off in OFFSETS:
        cut = lax.dynamic_slice_in_dim(cotangent[0], ((at["z"] - off) % 4) * classes, classes, 1)
        cot_blocks.append(cut if off == 0 else shift(cut, "z", -off))
        index = ((at["y"] * 4 + at["x"]) * 2 + at["c"]) * 4 + (at["z"] + off) % 4
        label_rows.append(lax.dynamic_slice_in_dim(labels, index, 1, 0))
    task_weight = samples / (3.0 * counts.astype(F32))
    column = jnp.arange(classes)
    column_task = (column >= 1).astype(jnp.int32) + (column >= 4).astype(jnp.int32)
    column_hot = (column_task[None, :] == jnp.arange(3)[:, None]).astype(F32)
    column_weight = jnp.sum(column_hot * task_weight[:, None], axis=0)
    label_mask = jnp.sum(
        jnp.concatenate(label_rows, 0).astype(F32)[:, :, None] * column_hot[None], axis=1
    )
    pred_grad = (
        jnp.stack(cot_blocks).astype(F32) * (label_mask * column_weight[None, :])[:, None, :]
    ).astype(BF).reshape(4 * tokens, classes)
    class_wide = (
        jnp.transpose(classifier).astype(F32)[:, None, :] * jnp.transpose(column_hot)[:, :, None]
    ).astype(BF).reshape(classes, 3 * hidden)

    weight_there, product, pred_grad, class_wide, gain, residual_wide = stage(
        weight_there, product, pred_grad, class_wide, gain, residual_wide
    )
    product = [
        part + dot(block[:, half:], weight_there, 1, 0)
        for part, block in zip(product, attn_blocks)
    ]
    product[1:] = [part.astype(BF) for part in product[1:]]
    product, late_piece, attn_blocks = stage(product, piece, attn_blocks)
    whole = lax.all_gather(late_piece, ("y", "x", "c", "z"), axis=0, tiled=True)
    parts = []
    for digit, off in enumerate(OFFSETS):
        parts.append(shift(product[digit], "z", off).astype(F32) if off else product[digit])
    pieces = []
    for i in range(4):
        off = (at["z"] - i) % 4
        near = jnp.where(off == 0, parts[0], parts[1])
        pieces.append(jnp.where((off == 0) | (off == 3), near, jnp.where(off == 1, parts[2], parts[3])))
    projected = jnp.concatenate(pieces, axis=1)
    stream = residual_wide + projected
    center = (stream - jnp.sum(stream, axis=1, keepdims=True) / width) * mask
    inverse = lax.rsqrt(jnp.sum(center * center, axis=1, keepdims=True) / width + 1e-06)
    normed = center * inverse
    features = (normed * gain).astype(BF)
    blocks = [features] + [shift(features, "z", -off) for off in OFFSETS[1:]]
    grads, activations, backs, returned = [], [], [], []
    for first, last in ((0, 1), (1, 3), (3, 4)):
        feats = jnp.concatenate(blocks[first:last], axis=0)
        pre_act = dot(feats, heads, 1, 0)
        act_grad = dot(pred_grad[first * tokens : last * tokens], class_wide, 1, 0)
        activations.append(jax.nn.silu(pre_act).astype(BF))
        grads.append((act_grad * silu_slope(pre_act)).astype(BF))
        if last < 4:
            grads[-1], blocks[last : last + 2] = stage(grads[-1], blocks[last : last + 2])
        back = dot(grads[-1], heads, 1, 1)
        for digit in range(first, last):
            part = back[(digit - first) * tokens : (digit - first + 1) * tokens]
            if digit:
                part = part.astype(BF)
                backs.append(part)
                part = shift(part, "z", OFFSETS[digit])
            returned.append(part)

    grads, backs, blocks, near = stage(grads, backs, blocks, returned[1:3])
    returned[1:3] = near
    deconv_all = dot(jnp.concatenate(blocks, axis=0), jnp.concatenate(grads, axis=0), 0, 0)
    core = at["c"] == 0
    deconv_there = jnp.where(core, deconv_all[half:], deconv_all[:half]).astype(BF)
    deconv_here = jnp.where(core, deconv_all[:half], deconv_all[half:]).astype(BF)
    returned, deconv_here, deconv_there, activations = stage(
        returned, deconv_here, deconv_there, activations
    )

    feature_grad = sum(part.astype(F32) for part in returned)
    scaled = feature_grad * gain
    stream_grad = inverse * (
        scaled
        - jnp.sum(scaled, axis=1, keepdims=True) / width
        - normed * (jnp.sum(scaled * normed, axis=1, keepdims=True) / width)
    ) * mask
    stream_bf = stream_grad.astype(BF)

    slabs = []
    for off in OFFSETS:
        slab = lax.dynamic_slice_in_dim(stream_bf, ((at["z"] - off) % 4) * cols, cols, 1)
        slabs.append(slab if off == 0 else shift(slab, "z", -off))
    deconv_there = exchange(deconv_there, "c", 1)
    class_part = dot(pred_grad, jnp.concatenate(activations, axis=0), 0, 0)
    class_part = class_part.reshape(classes, 3, hidden) * jnp.transpose(column_hot)[:, :, None]
    class_total = jnp.sum(class_part, axis=1)
    class_total = class_total + exchange(class_total, "c", 1)
    slabs, class_total, deconv_there = stage(slabs, class_total, deconv_there)

    part = dot(jnp.concatenate(attn_blocks, axis=0), jnp.concatenate(slabs, axis=0), 0, 0)
    part = part[:half] + exchange(part[half:].astype(BF), "c", 1).astype(F32)
    deconv_sum = deconv_here.astype(F32) + deconv_there.astype(F32)
    deconv_here, deconv_there = halves(deconv_sum, at["y"] // 2 % 2 == 0)
    deconv_there = exchange(deconv_there, "y", 2)
    class_total = class_total + exchange(class_total, "x", 1)
    part, class_total, stream_grad, stream_bf, deconv_here = stage(
        quarter(part), class_total, stream_grad, stream_bf, deconv_here
    )
    deconv_sum = deconv_here + deconv_there.astype(F32)

    part = collect(part, "x")
    class_total = class_total + exchange(class_total, "x", 2)
    class_total = class_total + exchange(class_total, "y", 1)
    high = lax.reduce_precision(stream_grad, 8, 7)
    middle = lax.reduce_precision(stream_grad - high, 8, 7)
    low = stream_grad - high - middle
    pieces = jnp.concatenate([high, middle, low], axis=0).astype(BF)
    pieces = dot(pieces, spread, 1, 1)
    grad_residual = pieces[:tokens] + pieces[tokens : 2 * tokens] + pieces[2 * tokens :]
    part, deconv_sum, class_total, grad_residual, stream_bf = stage(
        quarter(part), deconv_sum, class_total, grad_residual, stream_bf
    )

    part = collect(part, "y").reshape(4, LANE_ROWS, cols)
    deconv_sum = halve(deconv_sum, "y", 1, at["y"])
    class_total = class_total + exchange(class_total, "y", 2)
    class_total = class_total + exchange(class_total, "z", 1)
    part, deconv_sum, class_total, stream_bf = stage(part, deconv_sum, class_total, stream_bf)

    ordered = jnp.zeros((4, LANE_ROWS, cols), F32)
    for off in OFFSETS:
        strip = lax.dynamic_index_in_dim(part, (at["z"] - off) % 4, 0)
        if off:
            strip = shift(strip, "z", -off)
        ordered = lax.dynamic_update_slice_in_dim(ordered, strip, (at["z"] + off) % 4, 0)
    class_total = class_total + exchange(class_total, "z", 2)
    deconv_sum = halve(deconv_sum, "x", 2, at["x"])
    ordered, deconv_sum, class_total, stream_bf = stage(ordered, deconv_sum, class_total, stream_bf)

    deconv_sum = halve(deconv_sum, "x", 1, at["x"])
    attn_rows = dot(stream_bf, whole, 1, 1).astype(BF)
    grad_attention = dot(attn_rows, unpick, 1, 0).astype(BF)
    deconv_grad = jnp.transpose(deconv_sum[:rows_dp].reshape(rows_dp, 3, hidden), (1, 0, 2))
    weight_grad = jnp.transpose(ordered, (1, 0, 2)).reshape(LANE_ROWS, 2, groups // 2, pad_dp)
    weight_grad = jnp.transpose(weight_grad[:own_rows, :, :, :rows_dp], (0, 2, 1, 3))
    return (
        grad_residual[None],
        grad_attention[None],
        weight_grad.reshape(own_rows, width),
        deconv_grad,
        jnp.transpose(class_total),
    )


def solution(mesh):
    fine = Mesh(mesh.devices.reshape(4, 4, 2, 4), ("y", "x", "c", "z"))
    every = ("y", "x", "c", "z")
    batch = P(every, None, None)
    heads = P(None, ("y", "x", "c"), "z")
    in_specs = (batch, batch, P(every, None), P(), heads, P(), P(), P(), batch)
    out_specs = (batch, batch, P(every, None), heads, P())
    return jax.shard_map(
        per_device, mesh=fine, in_specs=in_specs, out_specs=out_specs, check_vma=False
    )
```

```python
import jax
import jax.numpy as jnp
from jax import lax
from jax.sharding import Mesh, PartitionSpec as P

BF = jnp.bfloat16
F32 = jnp.float32
OFFSETS = (0, 3, 1, 2)
LANE_ROWS = 16


def shift(value, axis, by):
    size = lax.axis_size(axis)
    return lax.ppermute(value, axis, [(i, (i + by) % size) for i in range(size)])


def exchange(value, axis, bit):
    return lax.ppermute(value, axis, [(i, i ^ bit) for i in range(lax.axis_size(axis))])


def gather_axis(piece, axis, dim):
    parts = [piece] + [shift(piece, axis, -off) for off in OFFSETS[1:]]
    return jnp.concatenate(parts, axis=dim)


def scatter_axis(value, axis):
    total = value[0]
    for digit, off in enumerate(OFFSETS[1:], 1):
        total = total + shift(value[digit].astype(BF), axis, off).astype(F32)
    return total


def collect(blocks, axis):
    total = blocks[0]
    for digit, off in enumerate(OFFSETS[1:], 1):
        total = total + shift(blocks[digit], axis, off).astype(F32)
    return total


def quarter(value):
    blocks = jnp.split(value, 4, axis=0)
    return [blocks[0]] + [block.astype(BF) for block in blocks[1:]]


def halves(value, low, dim=0):
    first, second = jnp.split(value, 2, axis=dim)
    return jnp.where(low, first, second), jnp.where(low, second, first).astype(BF)


def halve(value, axis, bit, index, dim=0):
    mine, theirs = halves(value, index // bit % 2 == 0, dim)
    return mine + exchange(theirs, axis, bit).astype(F32)


def dot(a, b, ca, cb):
    return lax.dot_general(a, b, (((ca,), (cb,)), ((), ())), preferred_element_type=F32)


def stage(*values):
    return lax.optimization_barrier(values)


def silu_slope(values):
    sigmoid_value = jax.nn.sigmoid(values)
    return sigmoid_value * (1.0 + values * (1.0 - sigmoid_value))


def per_device(
    residual, attn_output, out_weight, norm_gain, head_deconv, classifier, labels, counts, cotangent
):
    at = {name: lax.axis_index(name) for name in ("y", "x", "c", "z")}
    samples = labels.shape[0]
    attention = attn_output[0]
    tokens, width = attention.shape
    hidden, classes = classifier.shape
    rows_dp = head_deconv.shape[1]
    pad_dp = 64
    groups = width // rows_dp
    wide = groups * pad_dp
    half = wide // 2
    cols = wide // 4
    own_rows = out_weight.shape[0]

    padded = jnp.arange(wide)
    place = (padded // pad_dp % (groups // 2) * 2 + padded // half) * rows_dp + padded % pad_dp
    source = jnp.where(padded % pad_dp < rows_dp, place, -1)
    spread = (jnp.arange(width)[:, None] == source[None, :]).astype(BF)
    mask = (source >= 0).astype(F32)
    gain = jnp.transpose(norm_gain.reshape(groups // 2, 2, rows_dp), (1, 0, 2))
    gain = jnp.pad(gain, ((0, 0), (0, 0), (0, pad_dp - rows_dp))).reshape(wide)

    heads_local = jnp.pad(
        jnp.transpose(head_deconv, (1, 0, 2)).reshape(rows_dp, -1), ((0, pad_dp - rows_dp), (0, 0))
    )
    heads = lax.all_gather(heads_local, ("c", "y", "x"), axis=0, tiled=True)

    table = jnp.array(OFFSETS, jnp.int32)
    row = jnp.arange(128 * LANE_ROWS)
    sub = row % LANE_ROWS
    row_y = (at["y"] + table[row // (4 * LANE_ROWS) % 4]) % 4
    row_x = (at["x"] + table[row // (16 * LANE_ROWS) % 4]) % 4
    row_c = (at["c"] + row // (64 * LANE_ROWS)) % 2
    target = (((row_y * 4 + row_x) * 2 + row_c) * 4 + row // LANE_ROWS % 4) * own_rows + sub
    target = jnp.where(sub < own_rows, target, -1)
    pick = (jnp.arange(width)[:, None] == target[None, :]).astype(BF)

    natural = jnp.arange(128 * LANE_ROWS)
    natural = jnp.where(
        natural % LANE_ROWS < own_rows, natural // LANE_ROWS * own_rows + natural % LANE_ROWS, -1
    )
    unpick_column = natural

    cot_blocks = []
    label_rows = []
    for off in OFFSETS:
        cut = lax.dynamic_slice_in_dim(cotangent[0], ((at["z"] - off) % 4) * classes, classes, 1)
        cot_blocks.append(cut if off == 0 else shift(cut, "z", -off))
        index = ((at["y"] * 4 + at["x"]) * 2 + at["c"]) * 4 + (at["z"] + off) % 4
        label_rows.append(lax.dynamic_slice_in_dim(labels, index, 1, 0))
    task_weight = samples / (3.0 * counts.astype(F32))
    column = jnp.arange(classes)
    column_task = (column >= 1).astype(jnp.int32) + (column >= 4).astype(jnp.int32)
    column_hot = (column_task[None, :] == jnp.arange(3)[:, None]).astype(F32)
    column_weight = jnp.sum(column_hot * task_weight[:, None], axis=0)
    label_mask = jnp.sum(
        jnp.concatenate(label_rows, 0).astype(F32)[:, :, None] * column_hot[None], axis=1
    )
    pred_grad = (
        jnp.stack(cot_blocks).astype(F32) * (label_mask * column_weight[None, :])[:, None, :]
    ).astype(BF).reshape(4 * tokens, classes)
    class_wide = (
        jnp.transpose(classifier).astype(F32)[:, None, :] * jnp.transpose(column_hot)[:, :, None]
    ).astype(BF).reshape(classes, 3 * hidden)

    piece = jnp.pad(dot(out_weight, spread, 1, 0).astype(BF), ((0, LANE_ROWS - own_rows), (0, 0)))
    weight = jnp.zeros((4, LANE_ROWS, cols), BF)
    for off in OFFSETS:
        strip = lax.dynamic_slice_in_dim(piece, ((at["z"] - off) % 4) * cols, cols, 1)
        if off:
            strip = shift(strip, "z", -off)
        weight = lax.dynamic_update_slice_in_dim(weight, strip[None], (at["z"] + off) % 4, 0)
    weight = weight.reshape(4 * LANE_ROWS, cols)
    weight, attn_own = stage(weight, dot(attention, pick, 1, 0).astype(BF))
    weight = gather_axis(weight, "y", 0)
    attn_blocks = [attn_own, shift(attn_own, "z", -OFFSETS[1])]
    weight, attn_blocks, pred_grad, class_wide, gain = stage(
        weight, attn_blocks, pred_grad, class_wide, gain
    )
    weight = gather_axis(weight, "x", 0)
    attn_blocks += [shift(attn_blocks[0], "z", -off) for off in OFFSETS[2:]]
    weight, attn_blocks = stage(weight, attn_blocks)
    weight_there = exchange(weight, "c", 1)
    product = [dot(block[:, :half], weight, 1, 0) for block in attn_blocks]

    weight_there, product = stage(weight_there, product)
    product = [
        part + dot(block[:, half:], weight_there, 1, 0)
        for part, block in zip(product, attn_blocks)
    ]
    product[1:] = [part.astype(BF) for part in product[1:]]
    product, late_piece, attn_blocks, residual = stage(product, piece, attn_blocks, residual)
    residual_wide = dot(residual[0], spread, 1, 0)
    whole = lax.all_gather(late_piece, ("y", "x", "c", "z"), axis=0, tiled=True)
    parts = []
    for digit, off in enumerate(OFFSETS):
        parts.append(shift(product[digit], "z", off).astype(F32) if off else product[digit])
    pieces = []
    for i in range(4):
        off = (at["z"] - i) % 4
        near = jnp.where(off == 0, parts[0], parts[1])
        pieces.append(jnp.where((off == 0) | (off == 3), near, jnp.where(off == 1, parts[2], parts[3])))
    projected = jnp.concatenate(pieces, axis=1)
    stream = residual_wide + projected
    center = (stream - jnp.sum(stream, axis=1, keepdims=True) / width) * mask
    inverse = lax.rsqrt(jnp.sum(center * center, axis=1, keepdims=True) / width + 1e-06)
    normed = center * inverse
    features = (normed * gain).astype(BF)
    blocks = [features] + [shift(features, "z", -off) for off in OFFSETS[1:3]]
    grads, activations, backs, returned = [], [], [], []
    for first, last in ((0, 1), (1, 3), (3, 4)):
        feats = jnp.concatenate(blocks[first:last], axis=0)
        pre_act = dot(feats, heads, 1, 0)
        act_grad = dot(pred_grad[first * tokens : last * tokens], class_wide, 1, 0)
        activations.append(jax.nn.silu(pre_act).astype(BF))
        grads.append((act_grad * silu_slope(pre_act)).astype(BF))
        if first == 0:
            grads[0], features = stage(grads[0], features)
            blocks.append(shift(features, "z", -OFFSETS[3]))
            grads[0], blocks[1:3] = stage(grads[0], blocks[1:3])
        elif last == 3:
            grads[1], blocks[3] = stage(grads[1], blocks[3])
        back = dot(grads[-1], heads, 1, 1)
        for digit in range(first, last):
            part = back[(digit - first) * tokens : (digit - first + 1) * tokens]
            if digit:
                part = part.astype(BF)
                backs.append(part)
                part = shift(part, "z", OFFSETS[digit])
            returned.append(part)

    grads, backs, blocks, near = stage(grads, backs, blocks, returned[1:3])
    returned[1:3] = near
    deconv_all = dot(jnp.concatenate(blocks, axis=0), jnp.concatenate(grads, axis=0), 0, 0)
    core = at["c"] == 0
    deconv_there = jnp.where(core, deconv_all[half:], deconv_all[:half]).astype(BF)
    deconv_here = jnp.where(core, deconv_all[:half], deconv_all[half:]).astype(BF)
    returned, deconv_here, deconv_there, activations = stage(
        returned, deconv_here, deconv_there, activations
    )

    feature_grad = sum(part.astype(F32) for part in returned)
    scaled = feature_grad * gain
    stream_grad = inverse * (
        scaled
        - jnp.sum(scaled, axis=1, keepdims=True) / width
        - normed * (jnp.sum(scaled * normed, axis=1, keepdims=True) / width)
    ) * mask
    stream_bf = stream_grad.astype(BF)

    slabs = []
    for off in OFFSETS:
        slab = lax.dynamic_slice_in_dim(stream_bf, ((at["z"] - off) % 4) * cols, cols, 1)
        slabs.append(slab if off == 0 else shift(slab, "z", -off))
    deconv_there = exchange(deconv_there, "c", 1)
    class_part = dot(pred_grad, jnp.concatenate(activations, axis=0), 0, 0)
    class_part = class_part.reshape(classes, 3, hidden) * jnp.transpose(column_hot)[:, :, None]
    class_total = jnp.sum(class_part, axis=1)
    class_total = class_total + exchange(class_total, "c", 1)
    class_total = class_total + exchange(class_total, "y", 1)
    slabs, class_total, deconv_there = stage(slabs, class_total, deconv_there)

    part = dot(jnp.concatenate(attn_blocks, axis=0), jnp.concatenate(slabs, axis=0), 0, 0)
    part = part.astype(BF)
    part = part[:half].astype(F32) + exchange(part[half:], "c", 1).astype(F32)
    deconv_sum = deconv_here.astype(F32) + deconv_there.astype(F32)
    deconv_here, deconv_there = halves(deconv_sum, at["y"] // 2 % 2 == 0)
    deconv_there = exchange(deconv_there, "y", 2)
    class_total = class_total + exchange(class_total, "y", 2)
    part, class_total, stream_grad, stream_bf, deconv_here = stage(
        quarter(part), class_total, stream_grad, stream_bf, deconv_here
    )
    deconv_sum = deconv_here + deconv_there.astype(F32)

    part = collect(part, "x")
    class_total = class_total + exchange(class_total, "z", 1)
    class_total = class_total + exchange(class_total, "z", 2)
    high = lax.reduce_precision(stream_grad, 8, 7)
    middle = lax.reduce_precision(stream_grad - high, 8, 7)
    low = stream_grad - high - middle
    pieces = jnp.concatenate([high, middle, low], axis=0).astype(BF)
    pieces = dot(pieces, spread, 1, 1)
    grad_residual = pieces[:tokens] + pieces[tokens : 2 * tokens] + pieces[2 * tokens :]
    part, deconv_sum, class_total, grad_residual, stream_bf = stage(
        quarter(part), deconv_sum, class_total, grad_residual, stream_bf
    )

    part = collect(part, "y").reshape(4, LANE_ROWS, cols)
    deconv_sum = halve(deconv_sum.reshape(2, 2, 2 * pad_dp, -1), "x", 2, at["x"], 1)
    class_total = class_total + exchange(class_total, "x", 1)
    part, deconv_sum, class_total, stream_bf = stage(part, deconv_sum, class_total, stream_bf)

    ordered = jnp.zeros((4, LANE_ROWS, cols), F32)
    for off in OFFSETS:
        strip = lax.dynamic_index_in_dim(part, (at["z"] - off) % 4, 0)
        if off:
            strip = shift(strip, "z", -off)
        ordered = lax.dynamic_update_slice_in_dim(ordered, strip, (at["z"] + off) % 4, 0)
    class_total = class_total + exchange(class_total, "x", 2)
    deconv_sum = halve(deconv_sum, "y", 1, at["y"])
    ordered, deconv_sum, class_total, stream_bf = stage(ordered, deconv_sum, class_total, stream_bf)

    deconv_here, deconv_there = halves(deconv_sum.reshape(2 * pad_dp, -1), at["x"] % 2 == 0)
    deconv_there = exchange(deconv_there, "x", 1)
    attn_rows, unpick = stage(dot(stream_bf, whole, 1, 1).astype(BF), unpick_column)
    unpick = (unpick[:, None] == jnp.arange(width)[None, :]).astype(BF)
    grad_attention = dot(attn_rows, unpick, 1, 0).astype(BF)
    grad_attention, deconv_here = stage(grad_attention, deconv_here)
    deconv_sum = deconv_here + deconv_there.astype(F32)
    deconv_grad = jnp.transpose(deconv_sum[:rows_dp].reshape(rows_dp, 3, hidden), (1, 0, 2))
    weight_grad = jnp.transpose(ordered, (1, 0, 2)).reshape(LANE_ROWS, 2, groups // 2, pad_dp)
    weight_grad = jnp.transpose(weight_grad[:own_rows, :, :, :rows_dp], (0, 2, 1, 3))
    return (
        grad_residual[None],
        grad_attention[None],
        weight_grad.reshape(own_rows, width),
        deconv_grad,
        jnp.transpose(class_total),
    )


def solution(mesh):
    fine = Mesh(mesh.devices.reshape(4, 4, 2, 4), ("y", "x", "c", "z"))
    every = ("y", "x", "c", "z")
    batch = P(every, None, None)
    heads = P(None, ("y", "x", "c"), "z")
    in_specs = (batch, batch, P(every, None), P(), heads, P(), P(), P(), batch)
    out_specs = (batch, batch, P(every, None), heads, P())
    return jax.shard_map(
        per_device, mesh=fine, in_specs=in_specs, out_specs=out_specs, check_vma=False
    )
```

```python
import jax
import jax.numpy as jnp
from jax import lax
from jax.sharding import Mesh, PartitionSpec as P

BF = jnp.bfloat16
F32 = jnp.float32
OFFSETS = (0, 3, 1, 2)
LANE_ROWS = 16


def shift(value, axis, by):
    size = lax.axis_size(axis)
    return lax.ppermute(value, axis, [(i, (i + by) % size) for i in range(size)])


def exchange(value, axis, bit):
    return lax.ppermute(value, axis, [(i, i ^ bit) for i in range(lax.axis_size(axis))])


def gather_axis(piece, axis, dim):
    parts = [piece] + [shift(piece, axis, -off) for off in OFFSETS[1:]]
    return jnp.concatenate(parts, axis=dim)


def scatter_axis(value, axis):
    total = value[0]
    for digit, off in enumerate(OFFSETS[1:], 1):
        total = total + shift(value[digit].astype(BF), axis, off).astype(F32)
    return total


def collect(blocks, axis):
    total = blocks[0]
    for digit, off in enumerate(OFFSETS[1:], 1):
        total = total + shift(blocks[digit], axis, off).astype(F32)
    return total


def quarter(value):
    blocks = jnp.split(value, 4, axis=0)
    return [blocks[0]] + [block.astype(BF) for block in blocks[1:]]


def halves(value, low, dim=0):
    first, second = jnp.split(value, 2, axis=dim)
    return jnp.where(low, first, second), jnp.where(low, second, first).astype(BF)


def halve(value, axis, bit, index, dim=0):
    mine, theirs = halves(value, index // bit % 2 == 0, dim)
    return mine + exchange(theirs, axis, bit).astype(F32)


def dot(a, b, ca, cb):
    return lax.dot_general(a, b, (((ca,), (cb,)), ((), ())), preferred_element_type=F32)


def stage(*values):
    return lax.optimization_barrier(values)


def silu_slope(values):
    sigmoid_value = jax.nn.sigmoid(values)
    return sigmoid_value * (1.0 + values * (1.0 - sigmoid_value))


def per_device(
    residual, attn_output, out_weight, norm_gain, head_deconv, classifier, labels, counts, cotangent
):
    at = {name: lax.axis_index(name) for name in ("y", "x", "c", "z")}
    samples = labels.shape[0]
    attention = attn_output[0]
    tokens, width = attention.shape
    hidden, classes = classifier.shape
    rows_dp = head_deconv.shape[1]
    pad_dp = 64
    groups = width // rows_dp
    wide = groups * pad_dp
    half = wide // 2
    cols = wide // 4
    own_rows = out_weight.shape[0]

    padded = jnp.arange(wide)
    place = (padded // pad_dp % (groups // 2) * 2 + padded // half) * rows_dp + padded % pad_dp
    source = jnp.where(padded % pad_dp < rows_dp, place, -1)
    spread = (jnp.arange(width)[:, None] == source[None, :]).astype(BF)
    mask = (source >= 0).astype(F32)
    gain = jnp.transpose(norm_gain.reshape(groups // 2, 2, rows_dp), (1, 0, 2))
    gain = jnp.pad(gain, ((0, 0), (0, 0), (0, pad_dp - rows_dp))).reshape(wide)

    heads_local = jnp.pad(
        jnp.transpose(head_deconv, (1, 0, 2)).reshape(rows_dp, -1), ((0, pad_dp - rows_dp), (0, 0))
    )
    heads = lax.all_gather(heads_local, ("c", "y", "x"), axis=0, tiled=True)

    table = jnp.array(OFFSETS, jnp.int32)
    row = jnp.arange(128 * LANE_ROWS)
    sub = row % LANE_ROWS
    row_y = (at["y"] + table[row // (4 * LANE_ROWS) % 4]) % 4
    row_x = (at["x"] + table[row // (16 * LANE_ROWS) % 4]) % 4
    row_c = (at["c"] + row // (64 * LANE_ROWS)) % 2
    target = (((row_y * 4 + row_x) * 2 + row_c) * 4 + row // LANE_ROWS % 4) * own_rows + sub
    target = jnp.where(sub < own_rows, target, -1)
    pick = (jnp.arange(width)[:, None] == target[None, :]).astype(BF)

    cot_blocks = []
    label_rows = []
    for off in OFFSETS:
        cut = lax.dynamic_slice_in_dim(cotangent[0], ((at["z"] - off) % 4) * classes, classes, 1)
        cot_blocks.append(cut if off == 0 else shift(cut, "z", -off))
        index = ((at["y"] * 4 + at["x"]) * 2 + at["c"]) * 4 + (at["z"] + off) % 4
        label_rows.append(lax.dynamic_slice_in_dim(labels, index, 1, 0))
    task_weight = samples / (3.0 * counts.astype(F32))
    column = jnp.arange(classes)
    column_task = (column >= 1).astype(jnp.int32) + (column >= 4).astype(jnp.int32)
    column_hot = (column_task[None, :] == jnp.arange(3)[:, None]).astype(F32)
    column_weight = jnp.sum(column_hot * task_weight[:, None], axis=0)
    label_mask = jnp.sum(
        jnp.concatenate(label_rows, 0).astype(F32)[:, :, None] * column_hot[None], axis=1
    )
    pred_grad = (
        jnp.stack(cot_blocks).astype(F32) * (label_mask * column_weight[None, :])[:, None, :]
    ).astype(BF).reshape(4 * tokens, classes)
    class_wide = (
        jnp.transpose(classifier).astype(F32)[:, None, :] * jnp.transpose(column_hot)[:, :, None]
    ).astype(BF).reshape(classes, 3 * hidden)

    piece = jnp.pad(dot(out_weight, spread, 1, 0).astype(BF), ((0, LANE_ROWS - own_rows), (0, 0)))
    weight = jnp.zeros((4, LANE_ROWS, cols), BF)
    for off in OFFSETS:
        strip = lax.dynamic_slice_in_dim(piece, ((at["z"] - off) % 4) * cols, cols, 1)
        if off:
            strip = shift(strip, "z", -off)
        weight = lax.dynamic_update_slice_in_dim(weight, strip[None], (at["z"] + off) % 4, 0)
    weight = weight.reshape(4 * LANE_ROWS, cols)
    weight, attn_own = stage(weight, dot(attention, pick, 1, 0).astype(BF))
    weight = gather_axis(weight, "y", 0)
    attn_blocks = [attn_own, shift(attn_own, "z", -OFFSETS[1])]
    weight, attn_blocks, pred_grad, class_wide, gain = stage(
        weight, attn_blocks, pred_grad, class_wide, gain
    )
    weight = gather_axis(weight, "x", 0)
    attn_blocks += [shift(attn_blocks[0], "z", -off) for off in OFFSETS[2:]]
    weight, attn_blocks = stage(weight, attn_blocks)
    weight_there = exchange(weight, "c", 1)
    product = [dot(block[:, :half], weight, 1, 0) for block in attn_blocks]

    weight_there, product = stage(weight_there, product)
    product = [
        part + dot(block[:, half:], weight_there, 1, 0)
        for part, block in zip(product, attn_blocks)
    ]
    product[1:] = [part.astype(BF) for part in product[1:]]
    product, weights, attn_blocks, residual = stage(
        product, [weight, weight_there], attn_blocks, residual
    )
    residual_wide = dot(residual[0], spread, 1, 0)
    parts = []
    for digit, off in enumerate(OFFSETS):
        parts.append(shift(product[digit], "z", off).astype(F32) if off else product[digit])
    pieces = []
    for i in range(4):
        off = (at["z"] - i) % 4
        near = jnp.where(off == 0, parts[0], parts[1])
        pieces.append(jnp.where((off == 0) | (off == 3), near, jnp.where(off == 1, parts[2], parts[3])))
    projected = jnp.concatenate(pieces, axis=1)
    stream = residual_wide + projected
    center = (stream - jnp.sum(stream, axis=1, keepdims=True) / width) * mask
    inverse = lax.rsqrt(jnp.sum(center * center, axis=1, keepdims=True) / width + 1e-06)
    normed = center * inverse
    features = (normed * gain).astype(BF)
    blocks = [features] + [shift(features, "z", -off) for off in OFFSETS[1:3]]
    grads, activations, backs, returned = [], [], [], []
    for first, last in ((0, 1), (1, 3), (3, 4)):
        feats = jnp.concatenate(blocks[first:last], axis=0)
        pre_act = dot(feats, heads, 1, 0)
        act_grad = dot(pred_grad[first * tokens : last * tokens], class_wide, 1, 0)
        activations.append(jax.nn.silu(pre_act).astype(BF))
        grads.append((act_grad * silu_slope(pre_act)).astype(BF))
        if first == 0:
            grads[0], features = stage(grads[0], features)
            blocks.append(shift(features, "z", -OFFSETS[3]))
            grads[0], blocks[1:3] = stage(grads[0], blocks[1:3])
        back = dot(grads[-1], heads, 1, 1)
        for digit in range(first, last):
            part = back[(digit - first) * tokens : (digit - first + 1) * tokens]
            if digit:
                part = part.astype(BF)
                backs.append(part)
                part = shift(part, "z", OFFSETS[digit])
            returned.append(part)
        if last == 3:
            blocks[3], grads[1], *backs = stage(blocks[3], grads[1], *backs)

    class_part = dot(pred_grad, jnp.concatenate(activations, axis=0), 0, 0)
    class_part = class_part.reshape(classes, 3, hidden) * jnp.transpose(column_hot)[:, :, None]
    class_total = jnp.sum(class_part, axis=1)
    for axis, bit in (("c", 1), ("x", 1), ("x", 2)):
        class_total = class_total + exchange(class_total, axis, bit)
    grads, backs, blocks, near, class_total = stage(
        grads, backs, blocks, returned[1:3], class_total
    )
    returned[1:3] = near
    deconv_all = dot(jnp.concatenate(blocks, axis=0), jnp.concatenate(grads, axis=0), 0, 0)
    core = at["c"] == 0
    deconv_there = jnp.where(core, deconv_all[half:], deconv_all[:half]).astype(BF)
    deconv_here = jnp.where(core, deconv_all[:half], deconv_all[half:]).astype(BF)
    returned, deconv_here, deconv_there, class_total = stage(
        returned, deconv_here, deconv_there, class_total
    )

    feature_grad = sum(part.astype(F32) for part in returned)
    scaled = feature_grad * gain
    stream_grad = inverse * (
        scaled
        - jnp.sum(scaled, axis=1, keepdims=True) / width
        - normed * (jnp.sum(scaled * normed, axis=1, keepdims=True) / width)
    ) * mask
    stream_bf = stream_grad.astype(BF)

    slabs = []
    for off in OFFSETS:
        slab = lax.dynamic_slice_in_dim(stream_bf, ((at["z"] - off) % 4) * cols, cols, 1)
        slabs.append(slab if off == 0 else shift(slab, "z", -off))
    deconv_there = exchange(deconv_there, "c", 1)
    class_total = class_total + exchange(class_total, "y", 1)
    slabs, class_total, deconv_there = stage(slabs, class_total, deconv_there)

    even = at["z"] % 2 == 0
    kept = jnp.where(even, slabs[2], slabs[1])
    sent = jnp.where(even, slabs[1], slabs[2])
    part = dot(jnp.concatenate(attn_blocks, axis=0), jnp.concatenate(slabs, axis=0), 0, 0)
    part = part.astype(BF)
    part = part[:half].astype(F32) + exchange(part[half:], "c", 1).astype(F32)
    deconv_sum = deconv_here.astype(F32) + deconv_there.astype(F32)
    deconv_here, deconv_there = halves(deconv_sum, at["y"] // 2 % 2 == 0)
    deconv_there = exchange(deconv_there, "y", 2)
    class_total = class_total + exchange(class_total, "y", 2)
    rows = dot(
        jnp.concatenate([slabs[3], sent, slabs[0], kept], axis=0),
        jnp.concatenate(weights, axis=0),
        1,
        1,
    ).astype(BF)
    rows_there = exchange(rows[: 2 * tokens], "z", 2)
    part, class_total, stream_grad, deconv_here = stage(
        quarter(part), class_total, stream_grad, deconv_here
    )
    deconv_sum = deconv_here + deconv_there.astype(F32)

    part = collect(part, "x")
    high = lax.reduce_precision(stream_grad, 8, 7)
    middle = lax.reduce_precision(stream_grad - high, 8, 7)
    low = stream_grad - high - middle
    pieces = jnp.concatenate([high, middle, low], axis=0).astype(BF)
    pieces = dot(pieces, spread, 1, 1)
    grad_residual = pieces[:tokens] + pieces[tokens : 2 * tokens] + pieces[2 * tokens :]
    part, deconv_sum, rows_kept, grad_residual = stage(
        quarter(part), deconv_sum, rows[2 * tokens :], grad_residual
    )
    rows = rows_kept.astype(F32) + rows_there.astype(F32)
    rows_here, rows_there = rows[:tokens], rows[tokens:].astype(BF)

    part = collect(part, "y").reshape(4, LANE_ROWS, cols)
    deconv_sum = halve(deconv_sum.reshape(2, 2, 2 * pad_dp, -1), "x", 2, at["x"], 1)
    attn_rows = (rows_here + exchange(rows_there, "z", 1).astype(F32)).astype(BF)
    part, deconv_sum, attn_rows = stage(part, deconv_sum, attn_rows)

    ordered = jnp.zeros((4, LANE_ROWS, cols), F32)
    for off in OFFSETS:
        strip = lax.dynamic_index_in_dim(part, (at["z"] - off) % 4, 0)
        if off:
            strip = shift(strip, "z", -off)
        ordered = lax.dynamic_update_slice_in_dim(ordered, strip, (at["z"] + off) % 4, 0)
    class_total = class_total + exchange(class_total, "z", 1)
    deconv_sum = halve(deconv_sum, "y", 1, at["y"])
    ordered, deconv_sum, class_total, attn_rows = stage(ordered, deconv_sum, class_total, attn_rows)

    deconv_here, deconv_there = halves(deconv_sum.reshape(2 * pad_dp, -1), at["x"] % 2 == 0)
    deconv_there = exchange(deconv_there, "x", 1)
    class_there = exchange(class_total, "z", 2)
    grad_attention = dot(attn_rows, pick, 1, 1).astype(BF)
    grad_attention, deconv_here, class_total = stage(grad_attention, deconv_here, class_total)
    class_total = class_total + class_there
    deconv_sum = deconv_here + deconv_there.astype(F32)
    deconv_grad = jnp.transpose(deconv_sum[:rows_dp].reshape(rows_dp, 3, hidden), (1, 0, 2))
    weight_grad = jnp.transpose(ordered, (1, 0, 2)).reshape(LANE_ROWS, 2, groups // 2, pad_dp)
    weight_grad = jnp.transpose(weight_grad[:own_rows, :, :, :rows_dp], (0, 2, 1, 3))
    return (
        grad_residual[None],
        grad_attention[None],
        weight_grad.reshape(own_rows, width),
        deconv_grad,
        jnp.transpose(class_total),
    )


def solution(mesh):
    fine = Mesh(mesh.devices.reshape(4, 4, 2, 4), ("y", "x", "c", "z"))
    every = ("y", "x", "c", "z")
    batch = P(every, None, None)
    heads = P(None, ("y", "x", "c"), "z")
    in_specs = (batch, batch, P(every, None), P(), heads, P(), P(), P(), batch)
    out_specs = (batch, batch, P(every, None), heads, P())
    return jax.shard_map(
        per_device, mesh=fine, in_specs=in_specs, out_specs=out_specs, check_vma=False
    )
```

```python
import jax
import jax.numpy as jnp
from jax import lax
from jax.sharding import Mesh, PartitionSpec as P

BF = jnp.bfloat16
F32 = jnp.float32
OFFSETS = (0, 3, 1, 2)
LANE_ROWS = 16


def shift(value, axis, by):
    size = lax.axis_size(axis)
    return lax.ppermute(value, axis, [(i, (i + by) % size) for i in range(size)])


def exchange(value, axis, bit):
    return lax.ppermute(value, axis, [(i, i ^ bit) for i in range(lax.axis_size(axis))])


def gather_axis(piece, axis, dim):
    parts = [piece] + [shift(piece, axis, -off) for off in OFFSETS[1:]]
    return jnp.concatenate(parts, axis=dim)


def scatter_axis(value, axis):
    total = value[0]
    for digit, off in enumerate(OFFSETS[1:], 1):
        total = total + shift(value[digit].astype(BF), axis, off).astype(F32)
    return total


def collect(blocks, axis):
    total = blocks[0]
    for digit, off in enumerate(OFFSETS[1:], 1):
        total = total + shift(blocks[digit], axis, off).astype(F32)
    return total


def quarter(value):
    blocks = jnp.split(value, 4, axis=0)
    return [blocks[0]] + [block.astype(BF) for block in blocks[1:]]


def halves(value, low):
    first, second = jnp.split(value, 2, axis=0)
    return jnp.where(low, first, second), jnp.where(low, second, first).astype(BF)


def halve(value, axis, bit, index):
    mine, theirs = halves(value, index // bit % 2 == 0)
    return mine + exchange(theirs, axis, bit).astype(F32)


def dot(a, b, ca, cb):
    return lax.dot_general(a, b, (((ca,), (cb,)), ((), ())), preferred_element_type=F32)


def stage(*values):
    return lax.optimization_barrier(values)


def silu_slope(values):
    sigmoid_value = jax.nn.sigmoid(values)
    return sigmoid_value * (1.0 + values * (1.0 - sigmoid_value))


def per_device(
    residual, attn_output, out_weight, norm_gain, head_deconv, classifier, labels, counts, cotangent
):
    at = {name: lax.axis_index(name) for name in ("y", "x", "c", "z")}
    samples = labels.shape[0]
    attention = attn_output[0]
    tokens, width = attention.shape
    hidden, classes = classifier.shape
    rows_dp = head_deconv.shape[1]
    pad_dp = 64
    groups = width // rows_dp
    wide = groups * pad_dp
    half = wide // 2
    cols = wide // 4
    own_rows = out_weight.shape[0]

    padded = jnp.arange(wide)
    place = padded // pad_dp % 4 * 4 + padded // (4 * pad_dp) % 4
    place = (place * 2 + padded // half) * rows_dp + padded % pad_dp
    source = jnp.where(padded % pad_dp < rows_dp, place, -1)
    spread = (jnp.arange(width)[:, None] == source[None, :]).astype(BF)
    mask = (source >= 0).astype(F32)
    gain = jnp.transpose(norm_gain.reshape(4, 4, 2, rows_dp), (2, 1, 0, 3))
    gain = jnp.pad(gain.reshape(groups, rows_dp), ((0, 0), (0, pad_dp - rows_dp))).reshape(wide)

    heads_local = jnp.pad(
        jnp.transpose(head_deconv, (1, 0, 2)).reshape(rows_dp, -1), ((0, pad_dp - rows_dp), (0, 0))
    )
    heads = lax.all_gather(heads_local, ("c", "x", "y"), axis=0, tiled=True)

    table = jnp.array(OFFSETS, jnp.int32)
    row = jnp.arange(128 * LANE_ROWS)
    sub = row % LANE_ROWS
    row_x = (at["x"] + table[row // (4 * LANE_ROWS) % 4]) % 4
    row_y = (at["y"] + table[row // (16 * LANE_ROWS) % 4]) % 4
    row_c = (at["c"] + row // (64 * LANE_ROWS)) % 2
    target = (((row_y * 4 + row_x) * 2 + row_c) * 4 + row // LANE_ROWS % 4) * own_rows + sub
    target = jnp.where(sub < own_rows, target, -1)
    pick = (jnp.arange(width)[:, None] == target[None, :]).astype(BF)

    attn_own, out_weight, cotangent, labels, counts, classifier = stage(
        dot(attention, pick, 1, 0).astype(BF), out_weight, cotangent, labels, counts, classifier
    )
    attn_blocks = [attn_own, shift(attn_own, "z", -OFFSETS[1])]
    cot_blocks = []
    label_rows = []
    for off in OFFSETS:
        cut = lax.dynamic_slice_in_dim(cotangent[0], ((at["z"] - off) % 4) * classes, classes, 1)
        cot_blocks.append(cut if off == 0 else shift(cut, "z", -off))
        index = ((at["y"] * 4 + at["x"]) * 2 + at["c"]) * 4 + (at["z"] + off) % 4
        label_rows.append(lax.dynamic_slice_in_dim(labels, index, 1, 0))
    task_weight = samples / (3.0 * counts.astype(F32))
    column = jnp.arange(classes)
    column_task = (column >= 1).astype(jnp.int32) + (column >= 4).astype(jnp.int32)
    column_hot = (column_task[None, :] == jnp.arange(3)[:, None]).astype(F32)
    column_weight = jnp.sum(column_hot * task_weight[:, None], axis=0)
    label_mask = jnp.sum(
        jnp.concatenate(label_rows, 0).astype(F32)[:, :, None] * column_hot[None], axis=1
    )
    pred_grad = (
        jnp.stack(cot_blocks).astype(F32) * (label_mask * column_weight[None, :])[:, None, :]
    ).astype(BF).reshape(4 * tokens, classes)
    class_wide = (
        jnp.transpose(classifier).astype(F32)[:, None, :] * jnp.transpose(column_hot)[:, :, None]
    ).astype(BF).reshape(classes, 3 * hidden)
    piece = jnp.pad(dot(out_weight, spread, 1, 0).astype(BF), ((0, LANE_ROWS - own_rows), (0, 0)))
    weight = jnp.zeros((4, LANE_ROWS, cols), BF)
    for off in OFFSETS:
        strip = lax.dynamic_slice_in_dim(piece, ((at["z"] - off) % 4) * cols, cols, 1)
        if off:
            strip = shift(strip, "z", -off)
        weight = lax.dynamic_update_slice_in_dim(weight, strip[None], (at["z"] + off) % 4, 0)
    weight = weight.reshape(4 * LANE_ROWS, cols)
    weight, attn_blocks, pred_grad, class_wide = stage(weight, attn_blocks, pred_grad, class_wide)
    weight = gather_axis(weight, "x", 0)
    attn_blocks.append(shift(attn_blocks[0], "z", -OFFSETS[2]))
    weight, attn_blocks = stage(weight, attn_blocks)
    weight = gather_axis(weight, "y", 0)
    attn_blocks.append(shift(attn_blocks[0], "z", -OFFSETS[3]))
    weight, attn_blocks = stage(weight, attn_blocks)
    weight_there = exchange(weight, "c", 1)
    product = [dot(block[:, :half], weight, 1, 0) for block in attn_blocks]

    weight_there, product = stage(weight_there, product)
    product = [
        part + dot(block[:, half:], weight_there, 1, 0)
        for part, block in zip(product, attn_blocks)
    ]
    product[1:] = [part.astype(BF) for part in product[1:]]
    product, weights, attn_blocks, residual = stage(
        product, [weight, weight_there], attn_blocks, residual
    )
    residual_wide = dot(residual[0], spread, 1, 0)
    parts = []
    for digit, off in enumerate(OFFSETS):
        parts.append(shift(product[digit], "z", off).astype(F32) if off else product[digit])
    pieces = []
    for i in range(4):
        off = (at["z"] - i) % 4
        near = jnp.where(off == 0, parts[0], parts[1])
        pieces.append(jnp.where((off == 0) | (off == 3), near, jnp.where(off == 1, parts[2], parts[3])))
    projected = jnp.concatenate(pieces, axis=1)
    stream = residual_wide + projected
    center = (stream - jnp.sum(stream, axis=1, keepdims=True) / width) * mask
    inverse = lax.rsqrt(jnp.sum(center * center, axis=1, keepdims=True) / width + 1e-06)
    normed = center * inverse
    features = (normed * gain).astype(BF)
    blocks = [features] + [shift(features, "z", -off) for off in OFFSETS[1:3]]
    grads, activations, backs, returned = [], [], [], []
    for first, last in ((0, 1), (1, 3), (3, 4)):
        feats = jnp.concatenate(blocks[first:last], axis=0)
        pre_act = dot(feats, heads, 1, 0)
        act_grad = dot(pred_grad[first * tokens : last * tokens], class_wide, 1, 0)
        activations.append(jax.nn.silu(pre_act).astype(BF))
        grads.append((act_grad * silu_slope(pre_act)).astype(BF))
        if first == 0:
            grads[0], features = stage(grads[0], features)
            blocks.append(shift(features, "z", -OFFSETS[3]))
            grads[0], blocks[1:3] = stage(grads[0], blocks[1:3])
        back = dot(grads[-1], heads, 1, 1) if first else None
        for digit in range(first, last):
            if digit:
                part = back[(digit - first) * tokens : (digit - first + 1) * tokens].astype(BF)
                backs.append(part)
                returned.append(shift(part, "z", OFFSETS[digit]))
        if last == 3:
            blocks[3], grads[1], *backs = stage(blocks[3], grads[1], *backs)

    backs, activations, grads, blocks = stage(backs, activations, grads, blocks)
    class_part = dot(pred_grad, jnp.concatenate(activations, axis=0), 0, 0)
    class_part = class_part.reshape(classes, 3, hidden) * jnp.transpose(column_hot)[:, :, None]
    class_total = jnp.sum(class_part, axis=1)
    for axis, bit in (("c", 1), ("x", 1), ("x", 2)):
        class_total = class_total + exchange(class_total, axis, bit)
    own_back = dot(grads[0], heads, 1, 1)
    grads, blocks, near, class_total = stage(grads, blocks, returned[:2], class_total)
    returned[:2] = near
    deconv_all = dot(jnp.concatenate(blocks, axis=0), jnp.concatenate(grads, axis=0), 0, 0)
    core = at["c"] == 0
    deconv_there = jnp.where(core, deconv_all[half:], deconv_all[:half]).astype(BF)
    deconv_here = jnp.where(core, deconv_all[:half], deconv_all[half:]).astype(BF)
    returned, own_back, deconv_here, deconv_there, class_total = stage(
        returned, own_back, deconv_here, deconv_there, class_total
    )

    deconv_there = exchange(deconv_there, "c", 1)

    feature_grad = own_back + sum(part.astype(F32) for part in returned)
    scaled = feature_grad * gain
    stream_grad = inverse * (
        scaled
        - jnp.sum(scaled, axis=1, keepdims=True) / width
        - normed * (jnp.sum(scaled * normed, axis=1, keepdims=True) / width)
    ) * mask
    stream_bf = stream_grad.astype(BF)

    slabs = []
    for off in OFFSETS:
        slab = lax.dynamic_slice_in_dim(stream_bf, ((at["z"] - off) % 4) * cols, cols, 1)
        slabs.append(slab if off == 0 else shift(slab, "z", -off))
    deconv_sum = deconv_here.astype(F32) + deconv_there.astype(F32)
    deconv_here, deconv_there = halves(deconv_sum, at["x"] // 2 % 2 == 0)
    class_total = class_total + exchange(class_total, "y", 1)
    slabs, class_total, deconv_here, deconv_there = stage(
        slabs, class_total, deconv_here, deconv_there
    )
    deconv_there = exchange(deconv_there, "x", 2)

    even = at["z"] % 2 == 0
    kept = jnp.where(even, slabs[2], slabs[1])
    sent = jnp.where(even, slabs[1], slabs[2])
    part = dot(jnp.concatenate(attn_blocks, axis=0), jnp.concatenate(slabs, axis=0), 0, 0)
    part = part.astype(BF)
    part = part[:half].astype(F32) + exchange(part[half:], "c", 1).astype(F32)
    class_total = class_total + exchange(class_total, "y", 2)
    rows = dot(
        jnp.concatenate([slabs[3], sent, slabs[0], kept], axis=0),
        jnp.concatenate(weights, axis=0),
        1,
        1,
    ).astype(BF)
    rows_there = exchange(rows[: 2 * tokens], "z", 2)
    part, class_total, stream_grad, deconv_here = stage(
        quarter(part), class_total, stream_grad, deconv_here
    )
    deconv_sum = halve(deconv_here + deconv_there.astype(F32), "x", 1, at["x"])

    part = collect(part, "y")
    high = lax.reduce_precision(stream_grad, 8, 7)
    middle = lax.reduce_precision(stream_grad - high, 8, 7)
    low = stream_grad - high - middle
    pieces = jnp.concatenate([high, middle, low], axis=0).astype(BF)
    pieces = dot(pieces, spread, 1, 1)
    grad_residual = pieces[:tokens] + pieces[tokens : 2 * tokens] + pieces[2 * tokens :]
    part, deconv_sum, rows_kept, grad_residual = stage(
        quarter(part), deconv_sum, rows[2 * tokens :], grad_residual
    )
    rows = rows_kept.astype(F32) + rows_there.astype(F32)
    rows_here, rows_there = rows[:tokens], rows[tokens:].astype(BF)

    part = collect(part, "x").reshape(4, LANE_ROWS, cols)
    deconv_sum = halve(deconv_sum, "y", 2, at["y"])
    attn_rows = (rows_here + exchange(rows_there, "z", 1).astype(F32)).astype(BF)
    part, deconv_sum, attn_rows = stage(part, deconv_sum, attn_rows)

    ordered = jnp.zeros((4, LANE_ROWS, cols), F32)
    for off in OFFSETS:
        strip = lax.dynamic_index_in_dim(part, (at["z"] - off) % 4, 0)
        if off:
            strip = shift(strip, "z", -off)
        ordered = lax.dynamic_update_slice_in_dim(ordered, strip, (at["z"] + off) % 4, 0)
    class_total = class_total + exchange(class_total, "z", 1)
    deconv_sum = halve(deconv_sum, "y", 1, at["y"])
    ordered, deconv_sum, class_total, attn_rows = stage(ordered, deconv_sum, class_total, attn_rows)

    class_there = exchange(class_total, "z", 2)
    grad_attention = dot(attn_rows, pick, 1, 1).astype(BF)
    grad_attention, class_total = stage(grad_attention, class_total)
    class_total = class_total + class_there
    deconv_grad = jnp.transpose(deconv_sum[:rows_dp].reshape(rows_dp, 3, hidden), (1, 0, 2))
    weight_grad = jnp.transpose(ordered, (1, 0, 2)).reshape(LANE_ROWS, 2, 4, 4, pad_dp)
    weight_grad = jnp.transpose(weight_grad[:own_rows, ..., :rows_dp], (0, 3, 2, 1, 4))
    return (
        grad_residual[None],
        grad_attention[None],
        weight_grad.reshape(own_rows, width),
        deconv_grad,
        jnp.transpose(class_total),
    )


def solution(mesh):
    fine = Mesh(mesh.devices.reshape(4, 4, 2, 4), ("y", "x", "c", "z"))
    every = ("y", "x", "c", "z")
    batch = P(every, None, None)
    heads = P(None, ("y", "x", "c"), "z")
    in_specs = (batch, batch, P(every, None), P(), heads, P(), P(), P(), batch)
    out_specs = (batch, batch, P(every, None), heads, P())
    return jax.shard_map(
        per_device, mesh=fine, in_specs=in_specs, out_specs=out_specs, check_vma=False
    )
```

```python
import jax
import jax.numpy as jnp
from jax import lax
from jax.sharding import Mesh, PartitionSpec as P

BF = jnp.bfloat16
F32 = jnp.float32
OFFSETS = (0, 3, 1, 2)
LANE_ROWS = 16


def shift(value, axis, by):
    size = lax.axis_size(axis)
    return lax.ppermute(value, axis, [(i, (i + by) % size) for i in range(size)])


def exchange(value, axis, bit):
    return lax.ppermute(value, axis, [(i, i ^ bit) for i in range(lax.axis_size(axis))])


def gather_axis(piece, axis, dim):
    parts = [piece] + [shift(piece, axis, -off) for off in OFFSETS[1:]]
    return jnp.concatenate(parts, axis=dim)


def scatter_axis(value, axis):
    total = value[0]
    for digit, off in enumerate(OFFSETS[1:], 1):
        total = total + shift(value[digit].astype(BF), axis, off).astype(F32)
    return total


def collect(blocks, axis):
    total = blocks[0]
    for digit, off in enumerate(OFFSETS[1:], 1):
        total = total + shift(blocks[digit], axis, off).astype(F32)
    return total


def quarter(value):
    blocks = jnp.split(value, 4, axis=0)
    return [blocks[0]] + [block.astype(BF) for block in blocks[1:]]


def halves(value, low, dim=0):
    first, second = jnp.split(value, 2, axis=dim)
    return jnp.where(low, first, second), jnp.where(low, second, first).astype(BF)


def halve(value, axis, bit, index, dim=0):
    mine, theirs = halves(value, index // bit % 2 == 0, dim)
    return mine + exchange(theirs, axis, bit).astype(F32)


def dot(a, b, ca, cb):
    return lax.dot_general(a, b, (((ca,), (cb,)), ((), ())), preferred_element_type=F32)


def stage(*values):
    return lax.optimization_barrier(values)


def silu_slope(values):
    sigmoid_value = jax.nn.sigmoid(values)
    return sigmoid_value * (1.0 + values * (1.0 - sigmoid_value))


def per_device(
    residual, attn_output, out_weight, norm_gain, head_deconv, classifier, labels, counts, cotangent
):
    at = {name: lax.axis_index(name) for name in ("y", "x", "c", "z")}
    samples = labels.shape[0]
    attention = attn_output[0]
    tokens, width = attention.shape
    hidden, classes = classifier.shape
    rows_dp = head_deconv.shape[1]
    pad_dp = 64
    groups = width // rows_dp
    wide = groups * pad_dp
    half = wide // 2
    cols = wide // 4
    own_rows = out_weight.shape[0]

    padded = jnp.arange(wide)
    place = (padded // pad_dp % (groups // 2) * 2 + padded // half) * rows_dp + padded % pad_dp
    source = jnp.where(padded % pad_dp < rows_dp, place, -1)
    spread = (jnp.arange(width)[:, None] == source[None, :]).astype(BF)
    mask = (source >= 0).astype(F32)
    gain = jnp.transpose(norm_gain.reshape(groups // 2, 2, rows_dp), (1, 0, 2))
    gain = jnp.pad(gain, ((0, 0), (0, 0), (0, pad_dp - rows_dp))).reshape(wide)

    heads_local = jnp.pad(
        jnp.transpose(head_deconv, (1, 0, 2)).reshape(rows_dp, -1), ((0, pad_dp - rows_dp), (0, 0))
    )
    heads = lax.all_gather(heads_local, ("c", "y", "x"), axis=0, tiled=True)

    table = jnp.array(OFFSETS, jnp.int32)
    row = jnp.arange(128 * LANE_ROWS)
    sub = row % LANE_ROWS
    row_y = (at["y"] + table[row // (4 * LANE_ROWS) % 4]) % 4
    row_x = (at["x"] + table[row // (16 * LANE_ROWS) % 4]) % 4
    row_c = (at["c"] + row // (64 * LANE_ROWS)) % 2
    target = (((row_y * 4 + row_x) * 2 + row_c) * 4 + row // LANE_ROWS % 4) * own_rows + sub
    target = jnp.where(sub < own_rows, target, -1)
    pick = (jnp.arange(width)[:, None] == target[None, :]).astype(BF)

    cot_blocks = []
    label_rows = []
    for off in OFFSETS:
        cut = lax.dynamic_slice_in_dim(cotangent[0], ((at["z"] - off) % 4) * classes, classes, 1)
        cot_blocks.append(cut if off == 0 else shift(cut, "z", -off))
        index = ((at["y"] * 4 + at["x"]) * 2 + at["c"]) * 4 + (at["z"] + off) % 4
        label_rows.append(lax.dynamic_slice_in_dim(labels, index, 1, 0))
    task_weight = samples / (3.0 * counts.astype(F32))
    column = jnp.arange(classes)
    column_task = (column >= 1).astype(jnp.int32) + (column >= 4).astype(jnp.int32)
    column_hot = (column_task[None, :] == jnp.arange(3)[:, None]).astype(F32)
    column_weight = jnp.sum(column_hot * task_weight[:, None], axis=0)
    label_mask = jnp.sum(
        jnp.concatenate(label_rows, 0).astype(F32)[:, :, None] * column_hot[None], axis=1
    )
    pred_grad = (
        jnp.stack(cot_blocks).astype(F32) * (label_mask * column_weight[None, :])[:, None, :]
    ).astype(BF).reshape(4 * tokens, classes)
    class_wide = (
        jnp.transpose(classifier).astype(F32)[:, None, :] * jnp.transpose(column_hot)[:, :, None]
    ).astype(BF).reshape(classes, 3 * hidden)

    piece = jnp.pad(dot(out_weight, spread, 1, 0).astype(BF), ((0, LANE_ROWS - own_rows), (0, 0)))
    weight = jnp.zeros((4, LANE_ROWS, cols), BF)
    for off in OFFSETS:
        strip = lax.dynamic_slice_in_dim(piece, ((at["z"] - off) % 4) * cols, cols, 1)
        if off:
            strip = shift(strip, "z", -off)
        weight = lax.dynamic_update_slice_in_dim(weight, strip[None], (at["z"] + off) % 4, 0)
    weight = weight.reshape(4 * LANE_ROWS, cols)
    weight, attn_own = stage(weight, dot(attention, pick, 1, 0).astype(BF))
    weight = gather_axis(weight, "y", 0)
    attn_blocks = [attn_own, shift(attn_own, "z", -OFFSETS[1])]
    weight, attn_blocks, pred_grad, class_wide, gain = stage(
        weight, attn_blocks, pred_grad, class_wide, gain
    )
    weight = gather_axis(weight, "x", 0)
    attn_blocks += [shift(attn_blocks[0], "z", -off) for off in OFFSETS[2:]]
    weight, attn_blocks = stage(weight, attn_blocks)
    weight_there = exchange(weight, "c", 1)
    product = [dot(block[:, :half], weight, 1, 0) for block in attn_blocks]

    weight_there, product = stage(weight_there, product)
    product = [
        part + dot(block[:, half:], weight_there, 1, 0)
        for part, block in zip(product, attn_blocks)
    ]
    product[1:] = [part.astype(BF) for part in product[1:]]
    product, weights, attn_blocks, residual = stage(
        product, [weight, weight_there], attn_blocks, residual
    )
    residual_wide = dot(residual[0], spread, 1, 0)
    parts = []
    for digit, off in enumerate(OFFSETS):
        parts.append(shift(product[digit], "z", off).astype(F32) if off else product[digit])
    pieces = []
    for i in range(4):
        off = (at["z"] - i) % 4
        near = jnp.where(off == 0, parts[0], parts[1])
        pieces.append(jnp.where((off == 0) | (off == 3), near, jnp.where(off == 1, parts[2], parts[3])))
    projected = jnp.concatenate(pieces, axis=1)
    stream = residual_wide + projected
    center = (stream - jnp.sum(stream, axis=1, keepdims=True) / width) * mask
    inverse = lax.rsqrt(jnp.sum(center * center, axis=1, keepdims=True) / width + 1e-06)
    normed = center * inverse
    features = (normed * gain).astype(BF)
    blocks = [features] + [shift(features, "z", -off) for off in OFFSETS[1:3]]
    grads, activations, backs, returned = [], [], [], []
    for first, last in ((0, 1), (1, 3), (3, 4)):
        feats = jnp.concatenate(blocks[first:last], axis=0)
        pre_act = dot(feats, heads, 1, 0)
        act_grad = dot(pred_grad[first * tokens : last * tokens], class_wide, 1, 0)
        activations.append(jax.nn.silu(pre_act).astype(BF))
        grads.append((act_grad * silu_slope(pre_act)).astype(BF))
        if first == 0:
            grads[0], features = stage(grads[0], features)
            blocks.append(shift(features, "z", -OFFSETS[3]))
            grads[0], blocks[1:3] = stage(grads[0], blocks[1:3])
        back = dot(grads[-1], heads, 1, 1) if first else None
        for digit in range(first, last):
            if digit:
                part = back[(digit - first) * tokens : (digit - first + 1) * tokens].astype(BF)
                backs.append(part)
                returned.append(shift(part, "z", OFFSETS[digit]))
        if last == 3:
            blocks[3], grads[1], *backs = stage(blocks[3], grads[1], *backs)

    backs, activations, grads, blocks = stage(backs, activations, grads, blocks)
    class_part = dot(pred_grad, jnp.concatenate(activations, axis=0), 0, 0)
    class_part = class_part.reshape(classes, 3, hidden) * jnp.transpose(column_hot)[:, :, None]
    class_total = jnp.sum(class_part, axis=1)
    for axis, bit in (("c", 1), ("x", 1), ("x", 2)):
        class_total = class_total + exchange(class_total, axis, bit)
    own_back = dot(grads[0], heads, 1, 1)
    grads, blocks, near, class_total = stage(grads, blocks, returned[:2], class_total)
    returned[:2] = near
    deconv_all = dot(jnp.concatenate(blocks, axis=0), jnp.concatenate(grads, axis=0), 0, 0)
    core = at["c"] == 0
    deconv_there = jnp.where(core, deconv_all[half:], deconv_all[:half]).astype(BF)
    deconv_here = jnp.where(core, deconv_all[:half], deconv_all[half:]).astype(BF)
    returned, own_back, deconv_here, deconv_there, class_total = stage(
        returned, own_back, deconv_here, deconv_there, class_total
    )

    feature_grad = own_back + sum(part.astype(F32) for part in returned)
    scaled = feature_grad * gain
    stream_grad = inverse * (
        scaled
        - jnp.sum(scaled, axis=1, keepdims=True) / width
        - normed * (jnp.sum(scaled * normed, axis=1, keepdims=True) / width)
    ) * mask
    stream_bf = stream_grad.astype(BF)

    slabs = []
    for off in OFFSETS:
        slab = lax.dynamic_slice_in_dim(stream_bf, ((at["z"] - off) % 4) * cols, cols, 1)
        slabs.append(slab if off == 0 else shift(slab, "z", -off))
    deconv_there = exchange(deconv_there, "c", 1)
    class_total = class_total + exchange(class_total, "y", 1)
    slabs, class_total, deconv_there = stage(slabs, class_total, deconv_there)

    even = at["z"] % 2 == 0
    kept = jnp.where(even, slabs[2], slabs[1])
    sent = jnp.where(even, slabs[1], slabs[2])
    part = dot(jnp.concatenate(attn_blocks, axis=0), jnp.concatenate(slabs, axis=0), 0, 0)
    part = part.astype(BF)
    part = part[:half].astype(F32) + exchange(part[half:], "c", 1).astype(F32)
    deconv_sum = deconv_here.astype(F32) + deconv_there.astype(F32)
    deconv_here, deconv_there = halves(deconv_sum, at["y"] // 2 % 2 == 0)
    deconv_there = exchange(deconv_there, "y", 2)
    class_total = class_total + exchange(class_total, "y", 2)
    rows = dot(
        jnp.concatenate([slabs[3], sent, slabs[0], kept], axis=0),
        jnp.concatenate(weights, axis=0),
        1,
        1,
    ).astype(BF)
    rows_there = exchange(rows[: 2 * tokens], "z", 2)
    part, class_total, stream_grad, deconv_here = stage(
        quarter(part), class_total, stream_grad, deconv_here
    )
    deconv_sum = deconv_here + deconv_there.astype(F32)

    part = collect(part, "x")
    high = lax.reduce_precision(stream_grad, 8, 7)
    middle = lax.reduce_precision(stream_grad - high, 8, 7)
    low = stream_grad - high - middle
    pieces = jnp.concatenate([high, middle, low], axis=0).astype(BF)
    pieces = dot(pieces, spread, 1, 1)
    grad_residual = pieces[:tokens] + pieces[tokens : 2 * tokens] + pieces[2 * tokens :]
    part, deconv_sum, rows_kept, grad_residual = stage(
        quarter(part), deconv_sum, rows[2 * tokens :], grad_residual
    )
    rows = rows_kept.astype(F32) + rows_there.astype(F32)
    rows_here, rows_there = rows[:tokens], rows[tokens:].astype(BF)

    part = collect(part, "y").reshape(4, LANE_ROWS, cols)
    deconv_sum = halve(deconv_sum.reshape(2, 2, 2 * pad_dp, -1), "x", 2, at["x"], 1)
    attn_rows = (rows_here + exchange(rows_there, "z", 1).astype(F32)).astype(BF)
    part, deconv_sum, attn_rows = stage(part, deconv_sum, attn_rows)

    ordered = jnp.zeros((4, LANE_ROWS, cols), F32)
    for off in OFFSETS:
        strip = lax.dynamic_index_in_dim(part, (at["z"] - off) % 4, 0)
        if off:
            strip = shift(strip, "z", -off)
        ordered = lax.dynamic_update_slice_in_dim(ordered, strip, (at["z"] + off) % 4, 0)
    class_total = class_total + exchange(class_total, "z", 1)
    deconv_sum = halve(deconv_sum, "y", 1, at["y"])
    ordered, deconv_sum, class_total, attn_rows = stage(ordered, deconv_sum, class_total, attn_rows)

    deconv_here, deconv_there = halves(deconv_sum.reshape(2 * pad_dp, -1), at["x"] % 2 == 0)
    deconv_there = exchange(deconv_there, "x", 1)
    class_there = exchange(class_total, "z", 2)
    grad_attention = dot(attn_rows, pick, 1, 1).astype(BF)
    grad_attention, deconv_here, class_total = stage(grad_attention, deconv_here, class_total)
    class_total = class_total + class_there
    deconv_sum = deconv_here + deconv_there.astype(F32)
    deconv_grad = jnp.transpose(deconv_sum[:rows_dp].reshape(rows_dp, 3, hidden), (1, 0, 2))
    weight_grad = jnp.transpose(ordered, (1, 0, 2)).reshape(LANE_ROWS, 2, groups // 2, pad_dp)
    weight_grad = jnp.transpose(weight_grad[:own_rows, :, :, :rows_dp], (0, 2, 1, 3))
    return (
        grad_residual[None],
        grad_attention[None],
        weight_grad.reshape(own_rows, width),
        deconv_grad,
        jnp.transpose(class_total),
    )


def solution(mesh):
    fine = Mesh(mesh.devices.reshape(4, 4, 2, 4), ("y", "x", "c", "z"))
    every = ("y", "x", "c", "z")
    batch = P(every, None, None)
    heads = P(None, ("y", "x", "c"), "z")
    in_specs = (batch, batch, P(every, None), P(), heads, P(), P(), P(), batch)
    out_specs = (batch, batch, P(every, None), heads, P())
    return jax.shard_map(
        per_device, mesh=fine, in_specs=in_specs, out_specs=out_specs, check_vma=False
    )
```

```python
import jax
import jax.numpy as jnp
from jax import lax
from jax.sharding import Mesh, PartitionSpec as P

BF = jnp.bfloat16
F32 = jnp.float32
OFFSETS = (0, 3, 1, 2)
LANE_ROWS = 16


def shift(value, axis, by):
    size = lax.axis_size(axis)
    return lax.ppermute(value, axis, [(i, (i + by) % size) for i in range(size)])


def exchange(value, axis, bit):
    return lax.ppermute(value, axis, [(i, i ^ bit) for i in range(lax.axis_size(axis))])


def gather_axis(piece, axis, dim):
    parts = [piece] + [shift(piece, axis, -off) for off in OFFSETS[1:]]
    return jnp.concatenate(parts, axis=dim)


def scatter_axis(value, axis):
    total = value[0]
    for digit, off in enumerate(OFFSETS[1:], 1):
        total = total + shift(value[digit].astype(BF), axis, off).astype(F32)
    return total


def collect(blocks, axis):
    total = blocks[0]
    for digit, off in enumerate(OFFSETS[1:], 1):
        total = total + shift(blocks[digit], axis, off).astype(F32)
    return total


def quarter(value):
    blocks = jnp.split(value, 4, axis=0)
    return [blocks[0]] + [block.astype(BF) for block in blocks[1:]]


def halves(value, low, dim=0):
    first, second = jnp.split(value, 2, axis=dim)
    return jnp.where(low, first, second), jnp.where(low, second, first).astype(BF)


def halve(value, axis, bit, index, dim=0):
    mine, theirs = halves(value, index // bit % 2 == 0, dim)
    return mine + exchange(theirs, axis, bit).astype(F32)


def dot(a, b, ca, cb):
    return lax.dot_general(a, b, (((ca,), (cb,)), ((), ())), preferred_element_type=F32)


def stage(*values):
    return lax.optimization_barrier(values)


def silu_slope(values):
    sigmoid_value = jax.nn.sigmoid(values)
    return sigmoid_value * (1.0 + values * (1.0 - sigmoid_value))


def per_device(
    residual, attn_output, out_weight, norm_gain, head_deconv, classifier, labels, counts, cotangent
):
    at = {name: lax.axis_index(name) for name in ("y", "x", "c", "z")}
    samples = labels.shape[0]
    attention = attn_output[0]
    tokens, width = attention.shape
    hidden, classes = classifier.shape
    rows_dp = head_deconv.shape[1]
    pad_dp = 64
    groups = width // rows_dp
    wide = groups * pad_dp
    half = wide // 2
    cols = wide // 4
    own_rows = out_weight.shape[0]

    padded = jnp.arange(wide)
    place = (padded // pad_dp % (groups // 2) * 2 + padded // half) * rows_dp + padded % pad_dp
    source = jnp.where(padded % pad_dp < rows_dp, place, -1)
    spread = (jnp.arange(width)[:, None] == source[None, :]).astype(BF)
    mask = (source >= 0).astype(F32)
    gain = jnp.transpose(norm_gain.reshape(groups // 2, 2, rows_dp), (1, 0, 2))
    gain = jnp.pad(gain, ((0, 0), (0, 0), (0, pad_dp - rows_dp))).reshape(wide)

    heads_local = jnp.pad(
        jnp.transpose(head_deconv, (1, 0, 2)).reshape(rows_dp, -1), ((0, pad_dp - rows_dp), (0, 0))
    )
    heads = lax.all_gather(heads_local, ("c", "y", "x"), axis=0, tiled=True)

    table = jnp.array(OFFSETS, jnp.int32)
    row = jnp.arange(128 * LANE_ROWS)
    sub = row % LANE_ROWS
    row_y = (at["y"] + table[row // (4 * LANE_ROWS) % 4]) % 4
    row_x = (at["x"] + table[row // (16 * LANE_ROWS) % 4]) % 4
    row_c = (at["c"] + row // (64 * LANE_ROWS)) % 2
    target = (((row_y * 4 + row_x) * 2 + row_c) * 4 + row // LANE_ROWS % 4) * own_rows + sub
    target = jnp.where(sub < own_rows, target, -1)
    pick = (jnp.arange(width)[:, None] == target[None, :]).astype(BF)

    cot_blocks = []
    label_rows = []
    for off in OFFSETS:
        cut = lax.dynamic_slice_in_dim(cotangent[0], ((at["z"] - off) % 4) * classes, classes, 1)
        cot_blocks.append(cut if off == 0 else shift(cut, "z", -off))
        index = ((at["y"] * 4 + at["x"]) * 2 + at["c"]) * 4 + (at["z"] + off) % 4
        label_rows.append(lax.dynamic_slice_in_dim(labels, index, 1, 0))
    task_weight = samples / (3.0 * counts.astype(F32))
    column = jnp.arange(classes)
    column_task = (column >= 1).astype(jnp.int32) + (column >= 4).astype(jnp.int32)
    column_hot = (column_task[None, :] == jnp.arange(3)[:, None]).astype(F32)
    column_weight = jnp.sum(column_hot * task_weight[:, None], axis=0)
    label_mask = jnp.sum(
        jnp.concatenate(label_rows, 0).astype(F32)[:, :, None] * column_hot[None], axis=1
    )
    pred_grad = (
        jnp.stack(cot_blocks).astype(F32) * (label_mask * column_weight[None, :])[:, None, :]
    ).astype(BF).reshape(4 * tokens, classes)
    class_wide = (
        jnp.transpose(classifier).astype(F32)[:, None, :] * jnp.transpose(column_hot)[:, :, None]
    ).astype(BF).reshape(classes, 3 * hidden)

    piece = jnp.pad(dot(out_weight, spread, 1, 0).astype(BF), ((0, LANE_ROWS - own_rows), (0, 0)))
    weight = jnp.zeros((4, LANE_ROWS, cols), BF)
    for off in OFFSETS:
        strip = lax.dynamic_slice_in_dim(piece, ((at["z"] - off) % 4) * cols, cols, 1)
        if off:
            strip = shift(strip, "z", -off)
        weight = lax.dynamic_update_slice_in_dim(weight, strip[None], (at["z"] + off) % 4, 0)
    weight = weight.reshape(4 * LANE_ROWS, cols)
    weight, attn_own = stage(weight, dot(attention, pick, 1, 0).astype(BF))
    weight = gather_axis(weight, "y", 0)
    attn_blocks = [attn_own] + [shift(attn_own, "z", -off) for off in OFFSETS[1:3]]
    weight, attn_blocks, pred_grad, class_wide, gain = stage(
        weight, attn_blocks, pred_grad, class_wide, gain
    )
    weight = gather_axis(weight, "x", 0)
    attn_blocks.append(shift(attn_blocks[0], "z", -OFFSETS[3]))
    weight, attn_blocks = stage(weight, attn_blocks)
    weight_there = exchange(weight, "c", 1)
    product = [dot(block[:, :half], weight, 1, 0) for block in attn_blocks]

    weight_there, product = stage(weight_there, product)
    product = [
        part + dot(block[:, half:], weight_there, 1, 0)
        for part, block in zip(product, attn_blocks)
    ]
    product[1:] = [part.astype(BF) for part in product[1:]]
    product, weights, attn_blocks, residual = stage(
        product, [weight, weight_there], attn_blocks, residual
    )
    residual_wide = dot(residual[0], spread, 1, 0)
    parts = []
    for digit, off in enumerate(OFFSETS):
        parts.append(shift(product[digit], "z", off).astype(F32) if off else product[digit])
    pieces = []
    for i in range(4):
        off = (at["z"] - i) % 4
        near = jnp.where(off == 0, parts[0], parts[1])
        pieces.append(jnp.where((off == 0) | (off == 3), near, jnp.where(off == 1, parts[2], parts[3])))
    projected = jnp.concatenate(pieces, axis=1)
    stream = residual_wide + projected
    center = (stream - jnp.sum(stream, axis=1, keepdims=True) / width) * mask
    inverse = lax.rsqrt(jnp.sum(center * center, axis=1, keepdims=True) / width + 1e-06)
    normed = center * inverse
    features = (normed * gain).astype(BF)
    blocks = [features] + [shift(features, "z", -off) for off in OFFSETS[1:3]]
    grads, activations, backs, returned = [], [], [], []
    for first, last in ((0, 1), (1, 3), (3, 4)):
        feats = jnp.concatenate(blocks[first:last], axis=0)
        pre_act = dot(feats, heads, 1, 0)
        act_grad = dot(pred_grad[first * tokens : last * tokens], class_wide, 1, 0)
        activations.append(jax.nn.silu(pre_act).astype(BF))
        grads.append((act_grad * silu_slope(pre_act)).astype(BF))
        if first == 0:
            grads[0], features, blocks[1:3] = stage(grads[0], features, blocks[1:3])
            blocks.append(shift(features, "z", -OFFSETS[3]))
        back = dot(grads[-1], heads, 1, 1) if first else None
        for digit in range(first, last):
            if digit:
                part = back[(digit - first) * tokens : (digit - first + 1) * tokens].astype(BF)
                backs.append(part)
                returned.append(shift(part, "z", OFFSETS[digit]))
        if last == 3:
            blocks[3], grads[1], *backs = stage(blocks[3], grads[1], *backs)

    backs, activations, grads, blocks = stage(backs, activations, grads, blocks)
    class_part = dot(pred_grad, jnp.concatenate(activations, axis=0), 0, 0)
    class_part = class_part.reshape(classes, 3, hidden) * jnp.transpose(column_hot)[:, :, None]
    class_total = jnp.sum(class_part, axis=1)
    for axis, bit in (("c", 1), ("x", 1), ("x", 2)):
        class_total = class_total + exchange(class_total, axis, bit)
    own_back = dot(grads[0], heads, 1, 1)
    grads, blocks, near, class_total = stage(grads, blocks, returned[:2], class_total)
    returned[:2] = near
    deconv_all = dot(jnp.concatenate(blocks, axis=0), jnp.concatenate(grads, axis=0), 0, 0)
    core = at["c"] == 0
    deconv_there = jnp.where(core, deconv_all[half:], deconv_all[:half]).astype(BF)
    deconv_here = jnp.where(core, deconv_all[:half], deconv_all[half:]).astype(BF)
    returned, own_back, deconv_here, deconv_there, class_total = stage(
        returned, own_back, deconv_here, deconv_there, class_total
    )

    feature_grad = own_back + sum(part.astype(F32) for part in returned)
    scaled = feature_grad * gain
    stream_grad = inverse * (
        scaled
        - jnp.sum(scaled, axis=1, keepdims=True) / width
        - normed * (jnp.sum(scaled * normed, axis=1, keepdims=True) / width)
    ) * mask
    stream_bf = stream_grad.astype(BF)

    slabs = []
    for off in OFFSETS:
        slab = lax.dynamic_slice_in_dim(stream_bf, ((at["z"] - off) % 4) * cols, cols, 1)
        slabs.append(slab if off == 0 else shift(slab, "z", -off))
    deconv_there = exchange(deconv_there, "c", 1)
    class_total = class_total + exchange(class_total, "y", 1)
    slabs, class_total, deconv_there = stage(slabs, class_total, deconv_there)

    even = at["z"] % 2 == 0
    kept = jnp.where(even, slabs[2], slabs[1])
    sent = jnp.where(even, slabs[1], slabs[2])
    part = dot(jnp.concatenate(attn_blocks, axis=0), jnp.concatenate(slabs, axis=0), 0, 0)
    part = part.astype(BF)
    part = part[:half].astype(F32) + exchange(part[half:], "c", 1).astype(F32)
    deconv_sum = deconv_here.astype(F32) + deconv_there.astype(F32)
    deconv_here, deconv_there = halves(deconv_sum, at["y"] // 2 % 2 == 0)
    deconv_there = exchange(deconv_there, "y", 2)
    class_total = class_total + exchange(class_total, "y", 2)
    rows = dot(
        jnp.concatenate([slabs[3], sent, slabs[0], kept], axis=0),
        jnp.concatenate(weights, axis=0),
        1,
        1,
    ).astype(BF)
    rows_there = exchange(rows[: 2 * tokens], "z", 2)
    part, class_total, stream_grad, deconv_here = stage(
        quarter(part), class_total, stream_grad, deconv_here
    )
    deconv_sum = deconv_here + deconv_there.astype(F32)

    part = collect(part, "x")
    high = lax.reduce_precision(stream_grad, 8, 7)
    middle = lax.reduce_precision(stream_grad - high, 8, 7)
    low = stream_grad - high - middle
    pieces = jnp.concatenate([high, middle, low], axis=0).astype(BF)
    pieces = dot(pieces, spread, 1, 1)
    grad_residual = pieces[:tokens] + pieces[tokens : 2 * tokens] + pieces[2 * tokens :]
    part, deconv_sum, rows_kept, grad_residual = stage(
        quarter(part), deconv_sum, rows[2 * tokens :], grad_residual
    )
    rows = rows_kept.astype(F32) + rows_there.astype(F32)
    rows_here, rows_there = rows[:tokens], rows[tokens:].astype(BF)

    part = collect(part, "y").reshape(4, LANE_ROWS, cols)
    deconv_sum = halve(deconv_sum.reshape(2, 2, 2 * pad_dp, -1), "x", 2, at["x"], 1)
    attn_rows = (rows_here + exchange(rows_there, "z", 1).astype(F32)).astype(BF)
    part, deconv_sum, attn_rows = stage(part, deconv_sum, attn_rows)

    ordered = jnp.zeros((4, LANE_ROWS, cols), F32)
    for off in OFFSETS:
        strip = lax.dynamic_index_in_dim(part, (at["z"] - off) % 4, 0)
        if off:
            strip = shift(strip, "z", -off)
        ordered = lax.dynamic_update_slice_in_dim(ordered, strip, (at["z"] + off) % 4, 0)
    class_total = class_total + exchange(class_total, "z", 1)
    deconv_sum = halve(deconv_sum, "y", 1, at["y"])
    ordered, deconv_sum, class_total, attn_rows = stage(ordered, deconv_sum, class_total, attn_rows)

    deconv_here, deconv_there = halves(deconv_sum.reshape(2 * pad_dp, -1), at["x"] % 2 == 0)
    deconv_there = exchange(deconv_there, "x", 1)
    class_there = exchange(class_total, "z", 2)
    grad_attention = dot(attn_rows, pick, 1, 1).astype(BF)
    grad_attention, deconv_here, class_total = stage(grad_attention, deconv_here, class_total)
    class_total = class_total + class_there
    deconv_sum = deconv_here + deconv_there.astype(F32)
    deconv_grad = jnp.transpose(deconv_sum[:rows_dp].reshape(rows_dp, 3, hidden), (1, 0, 2))
    weight_grad = jnp.transpose(ordered, (1, 0, 2)).reshape(LANE_ROWS, 2, groups // 2, pad_dp)
    weight_grad = jnp.transpose(weight_grad[:own_rows, :, :, :rows_dp], (0, 2, 1, 3))
    return (
        grad_residual[None],
        grad_attention[None],
        weight_grad.reshape(own_rows, width),
        deconv_grad,
        jnp.transpose(class_total),
    )


def solution(mesh):
    fine = Mesh(mesh.devices.reshape(4, 4, 2, 4), ("y", "x", "c", "z"))
    every = ("y", "x", "c", "z")
    batch = P(every, None, None)
    heads = P(None, ("y", "x", "c"), "z")
    in_specs = (batch, batch, P(every, None), P(), heads, P(), P(), P(), batch)
    out_specs = (batch, batch, P(every, None), heads, P())
    return jax.shard_map(
        per_device, mesh=fine, in_specs=in_specs, out_specs=out_specs, check_vma=False
    )
```

```python
import jax
import jax.numpy as jnp
from jax import lax
from jax.sharding import Mesh, PartitionSpec as P

BF = jnp.bfloat16
F32 = jnp.float32
OFFSETS = (0, 3, 1, 2)
LANE_ROWS = 16


def shift(value, axis, by):
    size = lax.axis_size(axis)
    return lax.ppermute(value, axis, [(i, (i + by) % size) for i in range(size)])


def exchange(value, axis, bit):
    return lax.ppermute(value, axis, [(i, i ^ bit) for i in range(lax.axis_size(axis))])


def gather_axis(piece, axis, dim):
    parts = [piece] + [shift(piece, axis, -off) for off in OFFSETS[1:]]
    return jnp.concatenate(parts, axis=dim)


def scatter_axis(value, axis):
    total = value[0]
    for digit, off in enumerate(OFFSETS[1:], 1):
        total = total + shift(value[digit].astype(BF), axis, off).astype(F32)
    return total


def collect(blocks, axis):
    total = blocks[0]
    for digit, off in enumerate(OFFSETS[1:], 1):
        total = total + shift(blocks[digit], axis, off).astype(F32)
    return total


def quarter(value):
    blocks = jnp.split(value, 4, axis=0)
    return [blocks[0]] + [block.astype(BF) for block in blocks[1:]]


def halves(value, low, dim=0):
    first, second = jnp.split(value, 2, axis=dim)
    return jnp.where(low, first, second), jnp.where(low, second, first).astype(BF)


def halve(value, axis, bit, index, dim=0):
    mine, theirs = halves(value, index // bit % 2 == 0, dim)
    return mine + exchange(theirs, axis, bit).astype(F32)


def dot(a, b, ca, cb):
    return lax.dot_general(a, b, (((ca,), (cb,)), ((), ())), preferred_element_type=F32)


def stage(*values):
    return lax.optimization_barrier(values)


def silu_slope(values):
    sigmoid_value = jax.nn.sigmoid(values)
    return sigmoid_value * (1.0 + values * (1.0 - sigmoid_value))


def per_device(
    residual, attn_output, out_weight, norm_gain, head_deconv, classifier, labels, counts, cotangent
):
    at = {name: lax.axis_index(name) for name in ("y", "x", "c", "z")}
    samples = labels.shape[0]
    attention = attn_output[0]
    tokens, width = attention.shape
    hidden, classes = classifier.shape
    rows_dp = head_deconv.shape[1]
    pad_dp = 64
    groups = width // rows_dp
    wide = groups * pad_dp
    half = wide // 2
    cols = wide // 4
    own_rows = out_weight.shape[0]

    padded = jnp.arange(wide)
    place = (padded // pad_dp % (groups // 2) * 2 + padded // half) * rows_dp + padded % pad_dp
    source = jnp.where(padded % pad_dp < rows_dp, place, -1)
    spread = (jnp.arange(width)[:, None] == source[None, :]).astype(BF)
    mask = (source >= 0).astype(F32)
    gain = jnp.transpose(norm_gain.reshape(groups // 2, 2, rows_dp), (1, 0, 2))
    gain = jnp.pad(gain, ((0, 0), (0, 0), (0, pad_dp - rows_dp))).reshape(wide)

    heads_local = jnp.pad(
        jnp.transpose(head_deconv, (1, 0, 2)).reshape(rows_dp, -1), ((0, pad_dp - rows_dp), (0, 0))
    )
    heads = lax.all_gather(heads_local, ("c", "y", "x"), axis=0, tiled=True)

    table = jnp.array(OFFSETS, jnp.int32)
    row = jnp.arange(128 * LANE_ROWS)
    sub = row % LANE_ROWS
    row_y = (at["y"] + table[row // (4 * LANE_ROWS) % 4]) % 4
    row_x = (at["x"] + table[row // (16 * LANE_ROWS) % 4]) % 4
    row_c = (at["c"] + row // (64 * LANE_ROWS)) % 2
    target = (((row_y * 4 + row_x) * 2 + row_c) * 4 + row // LANE_ROWS % 4) * own_rows + sub
    target = jnp.where(sub < own_rows, target, -1)
    pick = (jnp.arange(width)[:, None] == target[None, :]).astype(BF)

    cot_blocks = []
    label_rows = []
    for off in OFFSETS:
        cut = lax.dynamic_slice_in_dim(cotangent[0], ((at["z"] - off) % 4) * classes, classes, 1)
        cot_blocks.append(cut if off == 0 else shift(cut, "z", -off))
        index = ((at["y"] * 4 + at["x"]) * 2 + at["c"]) * 4 + (at["z"] + off) % 4
        label_rows.append(lax.dynamic_slice_in_dim(labels, index, 1, 0))
    task_weight = samples / (3.0 * counts.astype(F32))
    column = jnp.arange(classes)
    column_task = (column >= 1).astype(jnp.int32) + (column >= 4).astype(jnp.int32)
    column_hot = (column_task[None, :] == jnp.arange(3)[:, None]).astype(F32)
    column_weight = jnp.sum(column_hot * task_weight[:, None], axis=0)
    label_mask = jnp.sum(
        jnp.concatenate(label_rows, 0).astype(F32)[:, :, None] * column_hot[None], axis=1
    )
    pred_grad = (
        jnp.stack(cot_blocks).astype(F32) * (label_mask * column_weight[None, :])[:, None, :]
    ).astype(BF).reshape(4 * tokens, classes)
    class_wide = (
        jnp.transpose(classifier).astype(F32)[:, None, :] * jnp.transpose(column_hot)[:, :, None]
    ).astype(BF).reshape(classes, 3 * hidden)

    piece = jnp.pad(dot(out_weight, spread, 1, 0).astype(BF), ((0, LANE_ROWS - own_rows), (0, 0)))
    weight = jnp.zeros((4, LANE_ROWS, cols), BF)
    for off in OFFSETS:
        strip = lax.dynamic_slice_in_dim(piece, ((at["z"] - off) % 4) * cols, cols, 1)
        if off:
            strip = shift(strip, "z", -off)
        weight = lax.dynamic_update_slice_in_dim(weight, strip[None], (at["z"] + off) % 4, 0)
    weight = weight.reshape(4 * LANE_ROWS, cols)
    weight, attn_own = stage(weight, dot(attention, pick, 1, 0).astype(BF))
    weight = gather_axis(weight, "y", 0)
    attn_blocks = [attn_own] + [shift(attn_own, "z", -off) for off in OFFSETS[1:3]]
    weight, attn_blocks, pred_grad, class_wide, gain = stage(
        weight, attn_blocks, pred_grad, class_wide, gain
    )
    weight = gather_axis(weight, "x", 0)
    attn_blocks.append(shift(attn_blocks[0], "z", -OFFSETS[3]))
    weight, attn_blocks = stage(weight, attn_blocks)
    weight_there = exchange(weight, "c", 1)
    product = [dot(block[:, :half], weight, 1, 0) for block in attn_blocks]

    weight_there, product = stage(weight_there, product)
    product = [
        part + dot(block[:, half:], weight_there, 1, 0)
        for part, block in zip(product, attn_blocks)
    ]
    product[1:] = [part.astype(BF) for part in product[1:]]
    product, weights, attn_blocks, residual = stage(
        product, [weight, weight_there], attn_blocks, residual
    )
    residual_wide = dot(residual[0], spread, 1, 0)
    parts = []
    for digit, off in enumerate(OFFSETS):
        parts.append(shift(product[digit], "z", off).astype(F32) if off else product[digit])
    pieces = []
    for i in range(4):
        off = (at["z"] - i) % 4
        near = jnp.where(off == 0, parts[0], parts[1])
        pieces.append(jnp.where((off == 0) | (off == 3), near, jnp.where(off == 1, parts[2], parts[3])))
    projected = jnp.concatenate(pieces, axis=1)
    stream = residual_wide + projected
    center = (stream - jnp.sum(stream, axis=1, keepdims=True) / width) * mask
    inverse = lax.rsqrt(jnp.sum(center * center, axis=1, keepdims=True) / width + 1e-06)
    normed = center * inverse
    features = (normed * gain).astype(BF)
    blocks = [features] + [shift(features, "z", -off) for off in OFFSETS[1:3]]
    grads, activations, backs, returned = [], [], [], []
    for first, last in ((0, 1), (1, 3), (3, 4)):
        feats = jnp.concatenate(blocks[first:last], axis=0)
        pre_act = dot(feats, heads, 1, 0)
        act_grad = dot(pred_grad[first * tokens : last * tokens], class_wide, 1, 0)
        activations.append(jax.nn.silu(pre_act).astype(BF))
        grads.append((act_grad * silu_slope(pre_act)).astype(BF))
        if first == 0:
            grads[0], features, blocks[1:3] = stage(grads[0], features, blocks[1:3])
            blocks.append(shift(features, "z", -OFFSETS[3]))
        back = dot(grads[-1], heads, 1, 1) if first else None
        for digit in range(first, last):
            if digit:
                part = back[(digit - first) * tokens : (digit - first + 1) * tokens].astype(BF)
                backs.append(part)
                returned.append(shift(part, "z", OFFSETS[digit]))
        if last == 3:
            blocks[3], grads[1], *backs = stage(blocks[3], grads[1], *backs)

    backs, activations, grads, blocks = stage(backs, activations, grads, blocks)
    class_part = dot(pred_grad, jnp.concatenate(activations, axis=0), 0, 0)
    class_part = class_part.reshape(classes, 3, hidden) * jnp.transpose(column_hot)[:, :, None]
    class_total = jnp.sum(class_part, axis=1)
    for axis, bit in (("c", 1), ("x", 1), ("x", 2)):
        class_total = class_total + exchange(class_total, axis, bit)
    own_back = dot(grads[0], heads, 1, 1)
    grads, blocks, near, class_total = stage(grads, blocks, returned[:2], class_total)
    returned[:2] = near
    deconv_all = dot(jnp.concatenate(blocks, axis=0), jnp.concatenate(grads, axis=0), 0, 0)
    core = at["c"] == 0
    deconv_there = jnp.where(core, deconv_all[half:], deconv_all[:half]).astype(BF)
    deconv_here = jnp.where(core, deconv_all[:half], deconv_all[half:]).astype(BF)
    returned, own_back, deconv_here, deconv_there, class_total = stage(
        returned, own_back, deconv_here, deconv_there, class_total
    )

    feature_grad = own_back + sum(part.astype(F32) for part in returned)
    scaled = feature_grad * gain
    stream_grad = inverse * (
        scaled
        - jnp.sum(scaled, axis=1, keepdims=True) / width
        - normed * (jnp.sum(scaled * normed, axis=1, keepdims=True) / width)
    ) * mask
    stream_bf = stream_grad.astype(BF)

    slabs = []
    for off in OFFSETS:
        slab = lax.dynamic_slice_in_dim(stream_bf, ((at["z"] - off) % 4) * cols, cols, 1)
        slabs.append(slab if off == 0 else shift(slab, "z", -off))
    deconv_there = exchange(deconv_there, "c", 1)
    class_total = class_total + exchange(class_total, "y", 1)
    slabs, class_total, deconv_there = stage(slabs, class_total, deconv_there)

    even = at["z"] % 2 == 0
    kept = jnp.where(even, slabs[2], slabs[1])
    sent = jnp.where(even, slabs[1], slabs[2])
    part = dot(jnp.concatenate(attn_blocks, axis=0), jnp.concatenate(slabs, axis=0), 0, 0)
    part = part.astype(BF)
    part = part[:half].astype(F32) + exchange(part[half:], "c", 1).astype(F32)
    deconv_sum = deconv_here.astype(F32) + deconv_there.astype(F32)
    deconv_here, deconv_there = halves(deconv_sum, at["y"] // 2 % 2 == 0)
    deconv_there = exchange(deconv_there, "y", 2)
    class_total = class_total + exchange(class_total, "y", 2)
    rows = dot(
        jnp.concatenate([slabs[3], sent, slabs[0], kept], axis=0),
        jnp.concatenate(weights, axis=0),
        1,
        1,
    ).astype(BF)
    rows_there = exchange(rows[: 2 * tokens], "z", 2)
    part, class_total, stream_grad, deconv_here = stage(
        quarter(part), class_total, stream_grad, deconv_here
    )
    deconv_sum = deconv_here + deconv_there.astype(F32)

    part = collect(part, "x")
    high = lax.reduce_precision(stream_grad, 8, 7)
    middle = lax.reduce_precision(stream_grad - high, 8, 7)
    low = stream_grad - high - middle
    pieces = jnp.concatenate([high, middle, low], axis=0).astype(BF)
    pieces = dot(pieces, spread, 1, 1)
    grad_residual = pieces[:tokens] + pieces[tokens : 2 * tokens] + pieces[2 * tokens :]
    part, deconv_sum, rows_kept, grad_residual = stage(
        quarter(part), deconv_sum, rows[2 * tokens :], grad_residual
    )
    rows = rows_kept.astype(F32) + rows_there.astype(F32)
    rows_here, rows_there = rows[:tokens], rows[tokens:].astype(BF)

    part = collect(part, "y").reshape(4, LANE_ROWS, cols)
    strips = jnp.split(deconv_sum, 4, axis=0)
    deconv_sum = jnp.concatenate([strips[0], strips[2], strips[1], strips[3]], axis=0)
    deconv_sum = halve(deconv_sum, "x", 2, at["x"])
    attn_rows = (rows_here + exchange(rows_there, "z", 1).astype(F32)).astype(BF)
    part, deconv_sum, attn_rows = stage(part, deconv_sum, attn_rows)

    ordered = jnp.zeros((4, LANE_ROWS, cols), F32)
    for off in OFFSETS:
        strip = lax.dynamic_index_in_dim(part, (at["z"] - off) % 4, 0)
        if off:
            strip = shift(strip, "z", -off)
        ordered = lax.dynamic_update_slice_in_dim(ordered, strip, (at["z"] + off) % 4, 0)
    class_total = class_total + exchange(class_total, "z", 1)
    deconv_sum = halve(deconv_sum, "y", 1, at["y"])
    ordered, deconv_sum, class_total, attn_rows = stage(ordered, deconv_sum, class_total, attn_rows)

    deconv_here, deconv_there = halves(deconv_sum.reshape(2 * pad_dp, -1), at["x"] % 2 == 0)
    deconv_there = exchange(deconv_there, "x", 1)
    class_there = exchange(class_total, "z", 2)
    grad_attention = dot(attn_rows, pick, 1, 1).astype(BF)
    grad_attention, deconv_here, class_total = stage(grad_attention, deconv_here, class_total)
    class_total = class_total + class_there
    deconv_sum = deconv_here + deconv_there.astype(F32)
    deconv_grad = jnp.transpose(deconv_sum[:rows_dp].reshape(rows_dp, 3, hidden), (1, 0, 2))
    weight_grad = jnp.transpose(ordered, (1, 0, 2)).reshape(LANE_ROWS, 2, groups // 2, pad_dp)
    weight_grad = jnp.transpose(weight_grad[:own_rows, :, :, :rows_dp], (0, 2, 1, 3))
    return (
        grad_residual[None],
        grad_attention[None],
        weight_grad.reshape(own_rows, width),
        deconv_grad,
        jnp.transpose(class_total),
    )


def solution(mesh):
    fine = Mesh(mesh.devices.reshape(4, 4, 2, 4), ("y", "x", "c", "z"))
    every = ("y", "x", "c", "z")
    batch = P(every, None, None)
    heads = P(None, ("y", "x", "c"), "z")
    in_specs = (batch, batch, P(every, None), P(), heads, P(), P(), P(), batch)
    out_specs = (batch, batch, P(every, None), heads, P())
    return jax.shard_map(
        per_device, mesh=fine, in_specs=in_specs, out_specs=out_specs, check_vma=False
    )
```

```python
import jax
import jax.numpy as jnp
from jax import lax
from jax.sharding import Mesh, PartitionSpec as P

BF = jnp.bfloat16
F32 = jnp.float32
OFFSETS = (0, 3, 1, 2)
LANE_ROWS = 16


def shift(value, axis, by):
    size = lax.axis_size(axis)
    return lax.ppermute(value, axis, [(i, (i + by) % size) for i in range(size)])


def exchange(value, axis, bit):
    return lax.ppermute(value, axis, [(i, i ^ bit) for i in range(lax.axis_size(axis))])


def gather_axis(piece, axis, dim):
    parts = [piece] + [shift(piece, axis, -off) for off in OFFSETS[1:]]
    return jnp.concatenate(parts, axis=dim)


def scatter_axis(value, axis):
    total = value[0]
    for digit, off in enumerate(OFFSETS[1:], 1):
        total = total + shift(value[digit].astype(BF), axis, off).astype(F32)
    return total


def collect(blocks, axis):
    total = blocks[0]
    for digit, off in enumerate(OFFSETS[1:], 1):
        total = total + shift(blocks[digit], axis, off).astype(F32)
    return total


def quarter(value):
    blocks = jnp.split(value, 4, axis=0)
    return [blocks[0]] + [block.astype(BF) for block in blocks[1:]]


def halves(value, low, dim=0):
    first, second = jnp.split(value, 2, axis=dim)
    return jnp.where(low, first, second), jnp.where(low, second, first).astype(BF)


def halve(value, axis, bit, index, dim=0):
    mine, theirs = halves(value, index // bit % 2 == 0, dim)
    return mine + exchange(theirs, axis, bit).astype(F32)


def dot(a, b, ca, cb):
    return lax.dot_general(a, b, (((ca,), (cb,)), ((), ())), preferred_element_type=F32)


def stage(*values):
    return lax.optimization_barrier(values)


def silu_slope(values):
    sigmoid_value = jax.nn.sigmoid(values)
    return sigmoid_value * (1.0 + values * (1.0 - sigmoid_value))


def per_device(
    residual, attn_output, out_weight, norm_gain, head_deconv, classifier, labels, counts, cotangent
):
    at = {name: lax.axis_index(name) for name in ("y", "x", "c", "z")}
    samples = labels.shape[0]
    attention = attn_output[0]
    tokens, width = attention.shape
    hidden, classes = classifier.shape
    rows_dp = head_deconv.shape[1]
    pad_dp = 64
    groups = width // rows_dp
    wide = groups * pad_dp
    half = wide // 2
    cols = wide // 4
    own_rows = out_weight.shape[0]

    padded = jnp.arange(wide)
    place = (padded // pad_dp % (groups // 2) * 2 + padded // half) * rows_dp + padded % pad_dp
    source = jnp.where(padded % pad_dp < rows_dp, place, -1)
    spread = (jnp.arange(width)[:, None] == source[None, :]).astype(BF)
    mask = (source >= 0).astype(F32)
    gain = jnp.transpose(norm_gain.reshape(groups // 2, 2, rows_dp), (1, 0, 2))
    gain = jnp.pad(gain, ((0, 0), (0, 0), (0, pad_dp - rows_dp))).reshape(wide)

    heads_local = jnp.pad(
        jnp.transpose(head_deconv, (1, 0, 2)).reshape(rows_dp, -1), ((0, pad_dp - rows_dp), (0, 0))
    )
    heads = lax.all_gather(heads_local, ("c", "y", "x"), axis=0, tiled=True)

    table = jnp.array(OFFSETS, jnp.int32)
    row = jnp.arange(128 * LANE_ROWS)
    sub = row % LANE_ROWS
    row_y = (at["y"] + table[row // (4 * LANE_ROWS) % 4]) % 4
    row_x = (at["x"] + table[row // (16 * LANE_ROWS) % 4]) % 4
    row_c = (at["c"] + row // (64 * LANE_ROWS)) % 2
    target = (((row_y * 4 + row_x) * 2 + row_c) * 4 + row // LANE_ROWS % 4) * own_rows + sub
    target = jnp.where(sub < own_rows, target, -1)
    pick = (jnp.arange(width)[:, None] == target[None, :]).astype(BF)

    cot_blocks = []
    label_rows = []
    for off in OFFSETS:
        cut = lax.dynamic_slice_in_dim(cotangent[0], ((at["z"] - off) % 4) * classes, classes, 1)
        cot_blocks.append(cut if off == 0 else shift(cut, "z", -off))
        index = ((at["y"] * 4 + at["x"]) * 2 + at["c"]) * 4 + (at["z"] + off) % 4
        label_rows.append(lax.dynamic_slice_in_dim(labels, index, 1, 0))
    task_weight = samples / (3.0 * counts.astype(F32))
    column = jnp.arange(classes)
    column_task = (column >= 1).astype(jnp.int32) + (column >= 4).astype(jnp.int32)
    column_hot = (column_task[None, :] == jnp.arange(3)[:, None]).astype(F32)
    column_weight = jnp.sum(column_hot * task_weight[:, None], axis=0)
    label_mask = jnp.sum(
        jnp.concatenate(label_rows, 0).astype(F32)[:, :, None] * column_hot[None], axis=1
    )
    pred_grad = (
        jnp.stack(cot_blocks).astype(F32) * (label_mask * column_weight[None, :])[:, None, :]
    ).astype(BF).reshape(4 * tokens, classes)
    class_wide = (
        jnp.transpose(classifier).astype(F32)[:, None, :] * jnp.transpose(column_hot)[:, :, None]
    ).astype(BF).reshape(classes, 3 * hidden)

    piece = jnp.pad(dot(out_weight, spread, 1, 0).astype(BF), ((0, LANE_ROWS - own_rows), (0, 0)))
    weight = jnp.zeros((4, LANE_ROWS, cols), BF)
    for off in OFFSETS:
        strip = lax.dynamic_slice_in_dim(piece, ((at["z"] - off) % 4) * cols, cols, 1)
        if off:
            strip = shift(strip, "z", -off)
        weight = lax.dynamic_update_slice_in_dim(weight, strip[None], (at["z"] + off) % 4, 0)
    weight = weight.reshape(4 * LANE_ROWS, cols)
    weight, attn_own = stage(weight, dot(attention, pick, 1, 0).astype(BF))
    weight = gather_axis(weight, "y", 0)
    attn_blocks = [attn_own] + [shift(attn_own, "z", -off) for off in OFFSETS[1:3]]
    weight, attn_blocks, pred_grad, class_wide, gain = stage(
        weight, attn_blocks, pred_grad, class_wide, gain
    )
    weight = gather_axis(weight, "x", 0)
    attn_blocks.append(shift(attn_blocks[0], "z", -OFFSETS[3]))
    weight, attn_blocks = stage(weight, attn_blocks)
    weight_there = exchange(weight, "c", 1)
    product = [dot(block[:, :half], weight, 1, 0) for block in attn_blocks]

    weight_there, product = stage(weight_there, product)
    product = [
        part + dot(block[:, half:], weight_there, 1, 0)
        for part, block in zip(product, attn_blocks)
    ]
    product[1:] = [part.astype(BF) for part in product[1:]]
    product, weights, attn_blocks, residual = stage(
        product, [weight, weight_there], attn_blocks, residual
    )
    residual_wide = dot(residual[0], spread, 1, 0)
    parts = []
    for digit, off in enumerate(OFFSETS):
        parts.append(shift(product[digit], "z", off).astype(F32) if off else product[digit])
    pieces = []
    for i in range(4):
        off = (at["z"] - i) % 4
        near = jnp.where(off == 0, parts[0], parts[1])
        pieces.append(jnp.where((off == 0) | (off == 3), near, jnp.where(off == 1, parts[2], parts[3])))
    projected = jnp.concatenate(pieces, axis=1)
    stream = residual_wide + projected
    center = (stream - jnp.sum(stream, axis=1, keepdims=True) / width) * mask
    inverse = lax.rsqrt(jnp.sum(center * center, axis=1, keepdims=True) / width + 1e-06)
    normed = center * inverse
    features = (normed * gain).astype(BF)
    blocks = [features] + [shift(features, "z", -off) for off in OFFSETS[1:3]]
    grads, activations, backs, returned = [], [], [], []
    for first, last in ((0, 1), (1, 3), (3, 4)):
        feats = jnp.concatenate(blocks[first:last], axis=0)
        pre_act = dot(feats, heads, 1, 0)
        act_grad = dot(pred_grad[first * tokens : last * tokens], class_wide, 1, 0)
        activations.append(jax.nn.silu(pre_act).astype(BF))
        grads.append((act_grad * silu_slope(pre_act)).astype(BF))
        if first == 0:
            grads[0], features, blocks[1:3] = stage(grads[0], features, blocks[1:3])
            blocks.append(shift(features, "z", -OFFSETS[3]))
        back = dot(grads[-1], heads, 1, 1) if first else None
        for digit in range(first, last):
            if digit:
                part = back[(digit - first) * tokens : (digit - first + 1) * tokens].astype(BF)
                backs.append(part)
                returned.append(shift(part, "z", OFFSETS[digit]))
        if last == 3:
            blocks[3], grads[1], *backs = stage(blocks[3], grads[1], *backs)

    backs, activations, grads, blocks = stage(backs, activations, grads, blocks)
    class_part = dot(pred_grad, jnp.concatenate(activations, axis=0), 0, 0)
    class_part = class_part.reshape(classes, 3, hidden) * jnp.transpose(column_hot)[:, :, None]
    class_total = jnp.sum(class_part, axis=1)
    for axis, bit in (("c", 1), ("x", 1), ("x", 2)):
        class_total = class_total + exchange(class_total, axis, bit)
    own_back = dot(grads[0], heads, 1, 1)
    grads, blocks, near, class_total = stage(grads, blocks, returned[:2], class_total)
    returned[:2] = near
    deconv_all = dot(jnp.concatenate(blocks, axis=0), jnp.concatenate(grads, axis=0), 0, 0)
    core = at["c"] == 0
    deconv_there = jnp.where(core, deconv_all[half:], deconv_all[:half]).astype(BF)
    deconv_here = jnp.where(core, deconv_all[:half], deconv_all[half:]).astype(BF)
    returned, own_back, deconv_here, deconv_there, class_total = stage(
        returned, own_back, deconv_here, deconv_there, class_total
    )

    feature_grad = own_back + sum(part.astype(F32) for part in returned)
    scaled = feature_grad * gain
    stream_grad = inverse * (
        scaled
        - jnp.sum(scaled, axis=1, keepdims=True) / width
        - normed * (jnp.sum(scaled * normed, axis=1, keepdims=True) / width)
    ) * mask
    stream_bf = stream_grad.astype(BF)

    slabs = []
    for off in OFFSETS:
        slab = lax.dynamic_slice_in_dim(stream_bf, ((at["z"] - off) % 4) * cols, cols, 1)
        slabs.append(slab if off == 0 else shift(slab, "z", -off))
    deconv_there = exchange(deconv_there, "c", 1)
    class_total = class_total + exchange(class_total, "y", 1)
    class_total = class_total + exchange(class_total, "z", 1)
    slabs, class_total, deconv_there = stage(slabs, class_total, deconv_there)

    even = at["z"] % 2 == 0
    kept = jnp.where(even, slabs[2], slabs[1])
    sent = jnp.where(even, slabs[1], slabs[2])
    part = dot(jnp.concatenate(attn_blocks, axis=0), jnp.concatenate(slabs, axis=0), 0, 0)
    part = part.astype(BF)
    part = part[:half].astype(F32) + exchange(part[half:], "c", 1).astype(F32)
    deconv_sum = deconv_here.astype(F32) + deconv_there.astype(F32)
    deconv_here, deconv_there = halves(deconv_sum, at["y"] // 2 % 2 == 0)
    deconv_there = exchange(deconv_there, "y", 2)
    class_total = class_total + exchange(class_total, "y", 2)
    rows = dot(
        jnp.concatenate([slabs[3], sent, slabs[0], kept], axis=0),
        jnp.concatenate(weights, axis=0),
        1,
        1,
    ).astype(BF)
    rows_there = exchange(rows[: 2 * tokens], "z", 2)
    part, class_total, stream_grad, deconv_here = stage(
        quarter(part), class_total, stream_grad, deconv_here
    )
    deconv_sum = deconv_here + deconv_there.astype(F32)

    part = collect(part, "x")
    high = lax.reduce_precision(stream_grad, 8, 7)
    middle = lax.reduce_precision(stream_grad - high, 8, 7)
    low = stream_grad - high - middle
    pieces = jnp.concatenate([high, middle, low], axis=0).astype(BF)
    pieces = dot(pieces, spread, 1, 1)
    grad_residual = pieces[:tokens] + pieces[tokens : 2 * tokens] + pieces[2 * tokens :]
    part, deconv_sum, rows_kept, grad_residual = stage(
        quarter(part), deconv_sum, rows[2 * tokens :], grad_residual
    )
    rows = rows_kept.astype(F32) + rows_there.astype(F32)
    rows_here, rows_there = rows[:tokens], rows[tokens:].astype(BF)

    part = collect(part, "y").reshape(4, LANE_ROWS, cols)
    strips = jnp.split(deconv_sum, 4, axis=0)
    deconv_sum = jnp.concatenate([strips[0], strips[2], strips[1], strips[3]], axis=0)
    deconv_sum = halve(deconv_sum, "x", 2, at["x"])
    attn_rows = (rows_here + exchange(rows_there, "z", 1).astype(F32)).astype(BF)
    part, deconv_sum, attn_rows = stage(part, deconv_sum, attn_rows)

    ordered = jnp.zeros((4, LANE_ROWS, cols), F32)
    for off in OFFSETS:
        strip = lax.dynamic_index_in_dim(part, (at["z"] - off) % 4, 0)
        if off:
            strip = shift(strip, "z", -off)
        ordered = lax.dynamic_update_slice_in_dim(ordered, strip, (at["z"] + off) % 4, 0)
    class_total = class_total + exchange(class_total, "z", 2)
    deconv_sum = halve(deconv_sum, "y", 1, at["y"])
    ordered, deconv_sum, class_total, attn_rows = stage(ordered, deconv_sum, class_total, attn_rows)

    deconv_here, deconv_there = halves(deconv_sum.reshape(2 * pad_dp, -1), at["x"] % 2 == 0)
    deconv_there = exchange(deconv_there, "x", 1)
    grad_attention = dot(attn_rows, pick, 1, 1).astype(BF)
    grad_attention, deconv_here, class_total = stage(grad_attention, deconv_here, class_total)
    deconv_sum = deconv_here + deconv_there.astype(F32)
    deconv_grad = jnp.transpose(deconv_sum[:rows_dp].reshape(rows_dp, 3, hidden), (1, 0, 2))
    weight_grad = jnp.transpose(ordered, (1, 0, 2)).reshape(LANE_ROWS, 2, groups // 2, pad_dp)
    weight_grad = jnp.transpose(weight_grad[:own_rows, :, :, :rows_dp], (0, 2, 1, 3))
    return (
        grad_residual[None],
        grad_attention[None],
        weight_grad.reshape(own_rows, width),
        deconv_grad,
        jnp.transpose(class_total),
    )


def solution(mesh):
    fine = Mesh(mesh.devices.reshape(4, 4, 2, 4), ("y", "x", "c", "z"))
    every = ("y", "x", "c", "z")
    batch = P(every, None, None)
    heads = P(None, ("y", "x", "c"), "z")
    in_specs = (batch, batch, P(every, None), P(), heads, P(), P(), P(), batch)
    out_specs = (batch, batch, P(every, None), heads, P())
    return jax.shard_map(
        per_device, mesh=fine, in_specs=in_specs, out_specs=out_specs, check_vma=False
    )
```
